256 devices in a mesh: dp: 8 (over y, core), feat: 32 (over x, z).
Axes of the slice: x: 4, y: 4, z: 8, core: 2. Of those that a mesh axis runs over, the one named last changes fastest.
Arguments:
- node_features: bfloat16 [1024, 65536], P('feat', 'dp'), may hold values from -6 to 6
- edge_tiles: bfloat16 [512, 4, 128, 128], P('dp'), may hold values from 0.019897461 to 1
- tile_source: int32 [512, 4], P('dp'), may hold values from 0 to 63, all different within a row
- tile_count: int32 [512], P('dp'), may hold values from 1 to 4, as said below
- drop_bits: int32 [512, 16], P(('dp', 'feat')), may hold values from -2147483648 to 2147483647, as said below
- cotangent: bfloat16 [65536, 512], P(('dp', 'feat')), may hold values from -0.0625 to 0.0625
- self_first: bfloat16 [1024, 512], replicated, may hold values from -0.1875 to 0.1875
- neigh_first: bfloat16 [1024, 512], replicated, may hold values from -0.1875 to 0.1875
- self_second: bfloat16 [512, 512], replicated, may hold values from -0.25 to 0.25
- neigh_second: bfloat16 [512, 512], replicated, may hold values from -0.25 to 0.25
Outputs:
- grad_self_first: float32 [1024, 512], P('feat')
- grad_neigh_first: float32 [1024, 512], P('feat')
- grad_self_second: float32 [512, 512], P('feat')
- grad_neigh_second: float32 [512, 512], P('feat')
The draws below stay inside these ranges and needn't reach their ends.
Inputs may be any that keep to these rules, and one draw needn't show every extreme that they name: `tile_source`: each row names 4 different source blocks; every block is named somewhere. `tile_count`: every draw has rows with one slot used and rows with all 4 used. `drop_bits`: any 32-bit pattern.
All inputs are finite; a program needn't handle non-finite values.
Results may differ from the reference program's by a relative error of at most 0.0085.
Values may be sent and summed in bfloat16 or wider, within the bound.
No kernel may reach another device: no remote copies, remote signals or barrier semaphores. Data moves between devices by JAX's collectives and lax.ppermute only.
A program may use at most 128 MiB of HBM per device.

```python
import math
import jax
import jax.numpy as jnp
from jax import lax

F = 1024
H = 512
TILE = 128
MAXT = 4
NBLK = 64
NODES = 8192
ALL_BLK = 512
N_DP = 8


def draw_tile_count(key, part):
    key = jax.random.fold_in(key, 11)
    counts = jax.random.randint(key, (ALL_BLK,), 1, MAXT + 1, dtype=jnp.int32)
    counts = counts.at[0::NBLK].set(MAXT)
    counts = counts.at[1::NBLK].set(1)
    return counts


def draw_drop_bits(key, part):
    key = jax.random.fold_in(key, 12)
    words = jax.random.randint(key, (ALL_BLK, H // 32), -2147483648, 2147483647, dtype=jnp.int32)
    words = words.at[0, 0].set(-2147483648)
    words = words.at[ALL_BLK - 1, H // 32 - 1].set(2147483647)
    return words


def levels(rng, shape, shards, smallest, largest):
    def one(position, shards_of):
        heights = jax.random.uniform(jax.random.fold_in(jax.random.fold_in(rng, 6), position), (shards_of,), jnp.float32, smallest / len(shards), largest / len(shards))
        return jnp.repeat(jnp.exp(heights), shape[position] // shards_of).reshape((-1,) + (1,) * (len(shape) - position - 1))

    gain = one(*shards[0])
    for cut in shards[1:]:
        gain = gain * one(*cut)
    return gain


def choose_distinct(rng, rows, count, top, lift):
    order = jax.random.permutation(jax.random.fold_in(rng, 1), count)
    boost = order
    for power in range(3):
        boost = boost * boost // count
    boost = boost * lift // count
    chance = jax.random.randint(jax.random.fold_in(rng, 2), (rows, count), 0, 4096) + boost
    sure = jax.random.permutation(jax.random.fold_in(rng, 3), rows)[jnp.arange(count) % rows]
    chance = jnp.where(jnp.arange(rows)[:, None] == sure[None, :], 1 << 14, chance)
    merit = chance * count + jnp.arange(count)
    return lax.top_k(merit.astype(jnp.int32), top)[1].astype(jnp.int32)


def gaussian(stream_key, extent, scale, bound, shards=(), held_as=jnp.bfloat16):
    factor_of = levels(stream_key, extent, shards, -0.22, 0.18) if shards else 1.0
    values = jax.random.normal(stream_key, extent, jnp.float32) * scale * factor_of
    return jnp.minimum(jnp.maximum(values, -bound), bound).astype(held_as)


def setup_inputs(seed: int = 0) -> dict:
    seeds = jax.random.split(jax.random.key(seed), 11)
    return {
        "node_features": gaussian(seeds[0], (F, N_DP * NODES), 1.0, 6.0, ((0, 32), (1, 8))),
        "edge_tiles": jnp.clip(jnp.exp(math.log(1.0) - 3.9171631 * jax.random.uniform(seeds[1], (ALL_BLK, MAXT, TILE, TILE), jnp.float32) ** levels(seeds[1], (ALL_BLK, MAXT, TILE, TILE), ((0, 8),), -0.2, 0.2)), 0.019897461, 1.0).astype(jnp.bfloat16),
        "tile_source": choose_distinct(seeds[2], ALL_BLK, NBLK, MAXT, 1024),
        "tile_count": draw_tile_count(jax.random.fold_in(seeds[10], 71), 0),
        "drop_bits": draw_drop_bits(jax.random.fold_in(seeds[10], 71), 0),
        "cotangent": gaussian(seeds[5], (N_DP * NODES, H), (1.0 / (N_DP * NODES) ** 0.5), 0.0625, ((0, 256),)),
        "self_first": gaussian(seeds[6], (F, H), F ** -0.5, 0.1875),
        "neigh_first": gaussian(seeds[7], (F, H), F ** -0.5, 0.1875),
        "self_second": gaussian(seeds[8], (H, H), H ** -0.5, 0.25),
        "neigh_second": gaussian(seeds[9], (H, H), H ** -0.5, 0.25),
    }


def unpack_keep(words):
    shifts = jnp.arange(32, dtype=jnp.int32)
    flags = jnp.bitwise_and(jnp.right_shift(words[:, :, None], shifts[None, None, :]), 1)
    return flags.reshape(words.shape[0], -1).astype(jnp.float32)

def one_replica(inputs):
    feats, tiles, source, counts, words, upstream, self_first, neigh_first, self_second, neigh_second = inputs
    blocks, slots, side, _ = tiles.shape
    node_count = blocks * side
    hidden_width = self_first.shape[1]
    live_float = (jnp.arange(slots)[None, :] < counts[:, None]).astype(jnp.float32)
    tiles_wide = tiles.astype(jnp.float32)
    degree = jnp.einsum('btrc,bt->br', tiles_wide, live_float)
    scaling = lax.rsqrt(degree)
    rows_major = feats.T
    source_rows = rows_major.reshape(blocks, side, -1)[source].astype(jnp.float32) * live_float[:, :, None, None]
    agg_one = (jnp.einsum('btrc,btcf->brf', tiles_wide, source_rows) * scaling[:, :, None]).reshape(node_count, -1).astype(jnp.bfloat16)
    pre_one = jnp.dot(rows_major, self_first, preferred_element_type=jnp.float32) + jnp.dot(agg_one, neigh_first, preferred_element_type=jnp.float32)
    keep_mask = jnp.repeat(unpack_keep(words), side, axis=0)
    sigma = jax.nn.sigmoid(pre_one)
    hidden = (pre_one * sigma * keep_mask * 2.0).astype(jnp.bfloat16)
    hidden_src = hidden.reshape(blocks, side, hidden_width)[source].astype(jnp.float32) * live_float[:, :, None, None]
    agg_two = (jnp.einsum('btrc,btch->brh', tiles_wide, hidden_src) * scaling[:, :, None]).reshape(node_count, hidden_width).astype(jnp.bfloat16)
    grad_self_second = jnp.dot(hidden.T, upstream, preferred_element_type=jnp.float32)
    grad_neigh_second = jnp.dot(agg_two.T, upstream, preferred_element_type=jnp.float32)
    back_scaled = (jnp.dot(upstream, neigh_second.T, preferred_element_type=jnp.float32) * scaling.reshape(node_count)[:, None]).astype(jnp.bfloat16)
    contrib = jnp.einsum('btrc,brh->btch', tiles_wide, back_scaled.reshape(blocks, side, hidden_width).astype(jnp.float32)) * live_float[:, :, None, None]
    back = jnp.zeros((blocks, side, hidden_width), jnp.float32).at[source].add(contrib).reshape(node_count, hidden_width)
    d_hidden = jnp.dot(upstream, self_second.T, preferred_element_type=jnp.float32) + back
    d_pre = (d_hidden * sigma * (1.0 + pre_one * (1.0 - sigma)) * keep_mask * 2.0).astype(jnp.bfloat16)
    grad_self_first = jnp.dot(feats, d_pre, preferred_element_type=jnp.float32)
    grad_neigh_first = jnp.dot(agg_one.T, d_pre, preferred_element_type=jnp.float32)
    return (grad_self_first, grad_neigh_first, grad_self_second, grad_neigh_second)

def reference(node_features, edge_tiles, tile_source, tile_count, drop_bits, cotangent, self_first, neigh_first, self_second, neigh_second):
    feats = node_features.reshape(F, N_DP, NODES).transpose(1, 0, 2)
    tiles = edge_tiles.reshape(N_DP, NBLK, MAXT, TILE, TILE)
    source = tile_source.reshape(N_DP, NBLK, MAXT)
    counts = tile_count.reshape(N_DP, NBLK)
    words = drop_bits.reshape(N_DP, NBLK, H // 32)
    upstream = cotangent.reshape(N_DP, NODES, H)

    def run(inputs):
        return one_replica(inputs + (self_first, neigh_first, self_second, neigh_second))
    grads = lax.map(run, (feats, tiles, source, counts, words, upstream))
    return (lax.optimization_barrier(jnp.sum(grads[0], axis=0)), lax.optimization_barrier(jnp.sum(grads[1], axis=0)), lax.optimization_barrier(jnp.sum(grads[2], axis=0)), lax.optimization_barrier(jnp.sum(grads[3], axis=0)))
```

```python
import functools

import jax
import jax.numpy as jnp
from jax import lax
from jax.experimental import pallas as pl
from jax.experimental.pallas import tpu as pltpu
from jax.sharding import PartitionSpec as P

BF = jnp.bfloat16
F32 = jnp.float32
STEP = 8
LAST = (((1,), (1,)), ((), ()))


def alive(count, slot):
    return jnp.where(slot < count, 1.0, 0.0).astype(F32)


def agg_kernel(source_ref, count_ref, x_ref, tiles_ref, agg_ref, scale_ref):
    slots, side = tiles_ref.shape[1], tiles_ref.shape[2]
    rows = x_ref.shape[0]
    for j in range(STEP):
        b = pl.program_id(0) * STEP + j
        count = count_ref[b]
        parts = []
        for t in range(slots):
            start = pl.multiple_of(source_ref[b, t] * side, side)
            x = x_ref[:, pl.ds(start, side)]
            x = jnp.concatenate([x, jnp.ones((16, side), BF)], axis=0)
            parts.append(x * jnp.full((rows + 16, side), alive(count, t), F32).astype(BF))
        lhs = jnp.concatenate(parts, axis=1)
        rhs = jnp.concatenate([tiles_ref[j, t] for t in range(slots)], axis=1)
        out = lax.dot_general(lhs, rhs, LAST, preferred_element_type=F32)
        scale = lax.rsqrt(out[rows : rows + 1])
        agg_ref[j // 2, :, (j % 2) * side : (j % 2 + 1) * side] = (out[:rows] * scale).astype(BF)
        scale_ref[j : j + 1] = scale


def back_kernel(source_ref, count_ref, g_ref, scale_ref, tiles_ref, agg_ref, out_ref, acc_ref):
    slots, side = tiles_ref.shape[1], tiles_ref.shape[2]
    rows = g_ref.shape[1]
    feats = agg_ref.shape[1]

    @pl.when(pl.program_id(0) == 0)
    def _():
        acc_ref[...] = jnp.zeros_like(acc_ref)

    for j in range(STEP):
        b = pl.program_id(0) * STEP + j
        count = count_ref[b]
        g = g_ref[j // 2, :, (j % 2) * side : (j % 2 + 1) * side].astype(F32)
        g = (g * scale_ref[j : j + 1]).astype(BF)
        rhs = jnp.concatenate([tiles_ref[j, t] for t in range(slots)], axis=1)
        out = jnp.dot(g, rhs, preferred_element_type=F32)
        for t in range(slots):
            src = source_ref[b, t]
            acc_ref[src] = acc_ref[src] + out[:, t * side : (t + 1) * side] * alive(count, t)

    @pl.when(pl.program_id(0) == pl.num_programs(0) - 1)
    def _():
        out_ref[:, :feats, :] = agg_ref[...]
        for o in range(out_ref.shape[0]):
            out_ref[o, feats:, :side] = acc_ref[2 * o].astype(BF)
            out_ref[o, feats:, side:] = acc_ref[2 * o + 1].astype(BF)


def grad_kernel(core_ref, one_ref, two_ref, g_ref, keep_ref, wsf_ref, wnf_ref, wss_ref, wns_ref, out_ref):
    owners, _, width = one_ref.shape
    feats = 32
    cols = two_ref.shape[1] - feats
    side = width // 2
    xt = one_ref[:, :feats, :].reshape(owners * feats, width)
    at = two_ref[:, :feats, :].reshape(owners * feats, width)
    qt = two_ref[:, feats:, :].reshape(owners * cols, width)
    g = g_ref[...]
    pre = jnp.dot(wsf_ref[...], xt, preferred_element_type=F32)
    pre = pre + jnp.dot(wnf_ref[...], at, preferred_element_type=F32)
    hidden_width = pre.shape[0]
    keep = jnp.concatenate(
        [
            jnp.broadcast_to(keep_ref[:, 0:1], (hidden_width, side)),
            jnp.broadcast_to(keep_ref[:, 1:2], (hidden_width, side)),
        ],
        axis=1,
    )
    sigma = jax.nn.sigmoid(pre)
    hidden = (pre * sigma * keep).astype(BF)
    back = lax.dot_general(wss_ref[...], g, LAST, preferred_element_type=F32)
    back = back + jnp.dot(wns_ref[...], qt, preferred_element_type=F32)
    d_pre = (back * sigma * (1.0 + pre * (1.0 - sigma)) * keep).astype(BF)
    core = core_ref[0]
    ys = out_ref.shape[1]
    for half in range(2):
        place = jnp.bitwise_xor(core, half)
        first = lax.dot_general(at if half else xt, d_pre, LAST, preferred_element_type=F32).astype(BF)
        if half:
            second = lax.dot_general(hidden, qt, LAST, preferred_element_type=F32).astype(BF)
        else:
            second = jnp.dot(hidden, g, preferred_element_type=F32).astype(BF)
        for y in range(ys):
            cut = slice(y * 128, (y + 1) * 128)
            out_ref[place, y, :, :feats, :] = first[:, cut].reshape(owners, feats, 128)
            out_ref[place, y, :, feats:, :] = second[:, cut].reshape(owners, cols, 128)


def params():
    return pltpu.CompilerParams(vmem_limit_bytes=48 * 1024 * 1024)


def smem():
    return pl.BlockSpec(memory_space=pltpu.SMEM)


def vmem():
    return pl.BlockSpec(memory_space=pltpu.VMEM)


def local(
    node_features,
    edge_tiles,
    tile_source,
    tile_count,
    drop_bits,
    cotangent,
    self_first,
    neigh_first,
    self_second,
    neigh_second,
    owners,
    replicas,
):
    blocks, slots, side, _ = edge_tiles.shape
    feats, nodes = node_features.shape
    width = nodes // owners
    hidden_width = self_first.shape[1]
    cols = hidden_width // owners
    steps = blocks // STEP
    own = STEP * side // width

    send = jnp.concatenate(
        [
            node_features.reshape(feats, owners, width).transpose(1, 0, 2),
            cotangent.T.reshape(owners, cols, width),
        ],
        axis=1,
    )
    one = lax.all_to_all(send, "feat", split_axis=0, concat_axis=0, tiled=True)

    tiles_spec = pl.BlockSpec((STEP, slots, side, side), lambda i: (i, 0, 0, 0))
    agg, scaling = pl.pallas_call(
        agg_kernel,
        grid=(steps,),
        in_specs=[smem(), smem(), pl.BlockSpec((feats, nodes), lambda i: (0, 0)), tiles_spec],
        out_specs=[
            pl.BlockSpec((own, feats, width), lambda i: (i, 0, 0)),
            pl.BlockSpec((STEP, side), lambda i: (i, 0)),
        ],
        out_shape=[
            jax.ShapeDtypeStruct((owners, feats, width), BF),
            jax.ShapeDtypeStruct((blocks, side), F32),
        ],
        compiler_params=params(),
        cost_estimate=pl.CostEstimate(flops=2 * 48 * 512 * 8192, bytes_accessed=10 << 20, transcendentals=0),
        name="agg",
    )(tile_source, tile_count, node_features, edge_tiles)

    send = pl.pallas_call(
        back_kernel,
        grid=(steps,),
        in_specs=[
            smem(),
            smem(),
            pl.BlockSpec((own, cols, width), lambda i: (i, 0, 0)),
            pl.BlockSpec((STEP, side), lambda i: (i, 0)),
            tiles_spec,
            pl.BlockSpec((owners, feats, width), lambda i: (0, 0, 0)),
        ],
        out_specs=pl.BlockSpec((owners, feats + cols, width), lambda i: (0, 0, 0)),
        out_shape=jax.ShapeDtypeStruct((owners, feats + cols, width), BF),
        scratch_shapes=[pltpu.VMEM((blocks, cols, side), F32)],
        compiler_params=params(),
        cost_estimate=pl.CostEstimate(flops=2 * 16 * 512 * 8192, bytes_accessed=10 << 20, transcendentals=0),
        name="back",
    )(tile_source, tile_count, one[:, feats:, :], scaling, edge_tiles, agg)
    two = lax.all_to_all(send, "feat", split_axis=0, concat_axis=0, tiled=True)

    shifts = jnp.arange(32, dtype=jnp.int32)
    bits = jnp.bitwise_and(jnp.right_shift(drop_bits[:, :, None], shifts), 1)
    keep = (bits.reshape(drop_bits.shape[0], hidden_width).astype(F32) * 2.0).T
    where = lax.axis_index("dp")
    core = where % 2
    ys = replicas // 2
    rows = feats + cols
    partial = pl.pallas_call(
        grad_kernel,
        in_specs=[smem()] + [vmem()] * 8,
        out_specs=vmem(),
        out_shape=jax.ShapeDtypeStruct((2, ys, owners, rows, 128), BF),
        compiler_params=params(),
        cost_estimate=pl.CostEstimate(flops=1600 << 20, bytes_accessed=9 << 20, transcendentals=1 << 17),
        name="grads",
    )(
        core.reshape(1),
        one,
        two,
        cotangent,
        keep,
        self_first.T,
        neigh_first.T,
        self_second,
        neigh_second,
    )

    other = lax.ppermute(partial[1], "dp", [(i, i ^ 1) for i in range(replicas)])
    pair = partial[0].astype(F32) + other.astype(F32)
    y = where // 2

    def of(k):
        return lax.dynamic_index_in_dim(pair, (y + k) % ys, 0, keepdims=False).astype(BF)

    def to(k):
        return [(i, ((i // 2 + k) % ys) * 2 + i % 2) for i in range(replicas)]

    total = of(0).astype(F32)
    for k in range(1, ys):
        total = total + lax.ppermute(of(k), "dp", to(k)).astype(F32)
    shares = lax.all_to_all(total.astype(BF), "feat", split_axis=0, concat_axis=0, tiled=True)
    share = jnp.sum(shares.astype(F32), axis=0)
    spread = jnp.broadcast_to(share[None], (replicas, rows, 128))
    spread = lax.all_to_all(spread, "dp", split_axis=0, concat_axis=0, tiled=True)
    spread = spread.reshape(ys, 2, rows, 128).transpose(1, 2, 0, 3).reshape(2, rows, hidden_width)
    return (spread[0, :feats], spread[1, :feats], spread[0, feats:], spread[1, feats:])


def solution(mesh):
    return jax.shard_map(
        functools.partial(local, owners=mesh.shape["feat"], replicas=mesh.shape["dp"]),
        mesh=mesh,
        in_specs=(
            P("feat", "dp"),
            P("dp", None, None, None),
            P("dp", None),
            P("dp"),
            P(("dp", "feat"), None),
            P(("dp", "feat"), None),
            P(),
            P(),
            P(),
            P(),
        ),
        out_specs=(P("feat", None), P("feat", None), P("feat", None), P("feat", None)),
        check_vma=False,
    )
```

```python
import functools

import jax
import jax.numpy as jnp
from jax import lax
from jax.experimental import pallas as pl
from jax.experimental.pallas import tpu as pltpu
from jax.sharding import PartitionSpec as P

BF = jnp.bfloat16
F32 = jnp.float32
STEP = 8
FEATS = 32
LAST = (((1,), (1,)), ((), ()))


def alive(count, slot):
    return jnp.where(slot < count, 1.0, 0.0).astype(F32)


def begin(pairs, sems):
    copies = [pltpu.make_async_copy(src, dst, sems.at[i]) for i, (src, dst) in enumerate(pairs)]
    for copy in copies:
        copy.start()
    return copies


def chunk(tiles_ref, held_ref, sems, i):
    part = pl.ds(i * STEP, STEP)
    return pltpu.make_async_copy(tiles_ref.at[part], held_ref.at[part], sems.at[i])


def prep_kernel(x_ref, g_ref, out_ref, x_held, g_held, sems):
    owners, rows, width = out_ref.shape
    copies = begin([(g_ref, g_held), (x_ref, x_held)], sems)
    copies[0].wait()
    out_ref[:, FEATS:, :] = g_held[...].T.reshape(owners, rows - FEATS, width)
    copies[1].wait()
    for o in range(owners):
        out_ref[o, :FEATS, :] = x_held[:, o * width : (o + 1) * width]


def agg_kernel(source_ref, count_ref, x_ref, tiles_ref, agg_ref, scale_ref, x_held, held_ref, x_sem, sems):
    blocks, slots, side, _ = held_ref.shape
    steps = blocks // STEP
    copies = begin([(x_ref, x_held)], x_sem)
    for i in range(steps):
        chunk(tiles_ref, held_ref, sems, i).start()
    copies[0].wait()

    @pl.loop(0, steps)
    def _(i):
        chunk(tiles_ref, held_ref, sems, i).wait()
        for j in range(STEP):
            b = i * STEP + j
            count = count_ref[b]
            parts = []
            for t in range(slots):
                start = pl.multiple_of(source_ref[b, t] * side, side)
                x = jnp.concatenate([x_held[:, pl.ds(start, side)], jnp.ones((16, side), BF)], axis=0)
                parts.append(x * jnp.full((FEATS + 16, side), alive(count, t), F32).astype(BF))
            lhs = jnp.concatenate(parts, axis=1)
            rhs = jnp.concatenate([held_ref[b, t] for t in range(slots)], axis=1)
            out = lax.dot_general(lhs, rhs, LAST, preferred_element_type=F32)
            scale = lax.rsqrt(out[FEATS : FEATS + 1])
            agg_ref[b // 2, :, (j % 2) * side : (j % 2 + 1) * side] = (out[:FEATS] * scale).astype(BF)
            scale_ref[pl.ds(b, 1)] = scale


def back_kernel(source_ref, count_ref, one_ref, scale_ref, tiles_ref, agg_ref, out_ref, acc_ref, held_ref, sems):
    blocks, slots, side, _ = held_ref.shape
    steps = blocks // STEP
    for i in range(steps):
        chunk(tiles_ref, held_ref, sems, i).start()
    acc_ref[...] = jnp.zeros_like(acc_ref)
    out_ref[:, :FEATS, :] = agg_ref[...]

    @pl.loop(0, steps)
    def _(i):
        chunk(tiles_ref, held_ref, sems, i).wait()
        for j in range(STEP):
            b = i * STEP + j
            count = count_ref[b]
            g = one_ref[b // 2, FEATS:, (j % 2) * side : (j % 2 + 1) * side].astype(F32)
            g = (g * scale_ref[pl.ds(b, 1)]).astype(BF)
            rhs = jnp.concatenate([held_ref[b, t] for t in range(slots)], axis=1)
            out = jnp.dot(g, rhs, preferred_element_type=F32)
            for t in range(slots):
                src = source_ref[b, t]
                acc_ref[src] = acc_ref[src] + out[:, t * side : (t + 1) * side] * alive(count, t)

    for o in range(out_ref.shape[0]):
        out_ref[o, FEATS:, :side] = acc_ref[2 * o].astype(BF)
        out_ref[o, FEATS:, side:] = acc_ref[2 * o + 1].astype(BF)


def upper(ref):
    owners, _, width = ref.shape
    return ref[:, :FEATS, :].reshape(owners * FEATS, width)


def lower(ref):
    owners, rows, width = ref.shape
    return ref[:, FEATS:, :].reshape(owners * (rows - FEATS), width)


def early_kernel(mine_ref, one_ref, wsf_ref, wss_ref, pre_ref, back_ref):
    pre_ref[...] = jnp.dot(wsf_ref[...], upper(one_ref), preferred_element_type=F32)
    back_ref[...] = jnp.dot(wss_ref[...], lower(mine_ref), preferred_element_type=F32)


def write_half(half, gt_ref, one_ref, two_ref, hidden, d_pre, out_ref):
    owners, rows, width = out_ref.shape
    if half:
        left, right = upper(two_ref), lower(two_ref)
    else:
        left, right = upper(one_ref), gt_ref[...].reshape(hidden.shape)
    first = lax.dot_general(left, d_pre, LAST, preferred_element_type=F32).astype(BF)
    out_ref[:, :FEATS, :] = first.reshape(owners, FEATS, width)
    second = lax.dot_general(hidden, right, LAST, preferred_element_type=F32).astype(BF)
    out_ref[:, FEATS:, :] = second.reshape(owners, rows - FEATS, width)


def send_kernel(
    core_ref,
    mine_ref,
    one_ref,
    two_ref,
    pre_ref,
    back_ref,
    keep_ref,
    wnf_ref,
    wns_ref,
    send_ref,
    hidden_ref,
    d_pre_ref,
    gt_held,
    pre_held,
    back_held,
    wnf_held,
    wns_held,
    sems,
):
    copies = begin(
        [
            (wnf_ref, wnf_held),
            (pre_ref, pre_held),
            (wns_ref, wns_held),
            (back_ref, back_held),
            (mine_ref.at[:, FEATS:, :], gt_held),
        ],
        sems,
    )
    copies[0].wait()
    pre = jnp.dot(wnf_held[...], upper(two_ref), preferred_element_type=F32)
    copies[1].wait()
    pre = pre + pre_held[...]
    hidden_width, width = pre.shape
    side = width // 2
    keep = jnp.concatenate(
        [
            jnp.broadcast_to(keep_ref[:, 0:1], (hidden_width, side)),
            jnp.broadcast_to(keep_ref[:, 1:2], (hidden_width, side)),
        ],
        axis=1,
    )
    sigma = jax.nn.sigmoid(pre)
    hidden_ref[...] = (pre * sigma * keep).astype(BF)
    slope = sigma * (1.0 + pre * (1.0 - sigma)) * keep
    copies[2].wait()
    back = jnp.dot(wns_held[...], lower(two_ref), preferred_element_type=F32)
    copies[3].wait()
    d_pre_ref[...] = ((back + back_held[...]) * slope).astype(BF)
    copies[4].wait()
    for core in range(2):

        @pl.when(core_ref[0] == core)
        def _():
            write_half(1 - core, gt_held, one_ref, two_ref, hidden_ref[...], d_pre_ref[...], send_ref)


def keep_kernel(core_ref, mine_ref, one_ref, two_ref, hidden_ref, d_pre_ref, keep_ref, gt_held, hidden, d_pre, sems):
    copies = begin(
        [(d_pre_ref, d_pre), (hidden_ref, hidden), (mine_ref.at[:, FEATS:, :], gt_held)], sems
    )
    for copy in copies:
        copy.wait()
    for core in range(2):

        @pl.when(core_ref[0] == core)
        def _():
            write_half(core, gt_held, one_ref, two_ref, hidden[...], d_pre[...], keep_ref)


def sum_one_kernel(x_ref, keep_ref, other_ref, send_a, send_b, own_a, own_b):
    x = x_ref[0]
    zs = keep_ref.shape[1] // 2
    for lo, send, own, first, later in ((0, send_a, own_a, 1, 3), (zs, send_b, own_b, 3, 1)):
        for out, slots in ((send, (first, 2)), (own, (0, later))):
            for i, slot in enumerate(slots):
                at = jnp.bitwise_xor(x, slot)
                a = keep_ref[at, lo : lo + zs].astype(F32)
                out[i] = (a + other_ref[at, lo : lo + zs].astype(F32)).astype(BF)


def sum_two_kernel(own_a, own_b, got_a, got_b, send_a, send_b, out_ref):
    zs = own_a.shape[1]
    for own, got, send, lo in ((own_a, got_a, send_a, 0), (own_b, got_b, send_b, zs)):
        send[...] = (own[1].astype(F32) + got[1].astype(F32)).astype(BF)
        out_ref[lo : lo + zs] = (own[0].astype(F32) + got[0].astype(F32)).astype(BF)


def sum_three_kernel(own_ref, got_a, got_b, out_ref):
    zs = got_a.shape[0]
    for got, lo in ((got_a, 0), (got_b, zs)):
        out_ref[lo : lo + zs] = (own_ref[lo : lo + zs].astype(F32) + got[...].astype(F32)).astype(BF)


def place_kernel(core_ref, own_ref, other_ref, *outs):
    for core in range(2):

        @pl.when(core_ref[0] == core)
        def _():
            for half in range(2):
                src = own_ref if half == core else other_ref
                outs[half][...] = src[:FEATS]
                outs[2 + half][...] = src[FEATS:]


SMEM = pl.BlockSpec(memory_space=pltpu.SMEM)
VMEM = pl.BlockSpec(memory_space=pltpu.VMEM)
HBM = pl.BlockSpec(memory_space=pltpu.HBM)
DMA = pltpu.SemaphoreType.DMA


def call(kernel, name, ins, outs, scratch=(), flops=0, size=1 << 20):
    run = pl.pallas_call(
        kernel,
        in_specs=list(ins),
        out_specs=[VMEM] * len(outs),
        out_shape=[jax.ShapeDtypeStruct(*o) for o in outs],
        scratch_shapes=list(scratch),
        compiler_params=pltpu.CompilerParams(vmem_limit_bytes=24 << 20),
        cost_estimate=pl.CostEstimate(flops=flops, bytes_accessed=size, transcendentals=0),
        name=name,
    )

    def apply(*args):
        return run(
            *(
                pltpu.with_memory_space_constraint(a, pltpu.HBM) if spec is HBM else a
                for a, spec in zip(args, ins, strict=True)
            )
        )

    return apply


def local(
    node_features,
    edge_tiles,
    tile_source,
    tile_count,
    drop_bits,
    cotangent,
    self_first,
    neigh_first,
    self_second,
    neigh_second,
    owners,
    replicas,
):
    blocks, slots, side, _ = edge_tiles.shape
    feats, nodes = node_features.shape
    width = nodes // owners
    hidden_width = self_first.shape[1]
    cols = hidden_width // owners
    rows = feats + cols
    steps = blocks // STEP
    exchange = functools.partial(lax.all_to_all, axis_name="feat", split_axis=0, concat_axis=0, tiled=True)

    (mine,) = call(
        prep_kernel,
        "prep",
        [HBM] * 2,
        [((owners, rows, width), BF)],
        [pltpu.VMEM((feats, nodes), BF), pltpu.VMEM((width, hidden_width), BF), DMA((2,))],
    )(node_features, cotangent)
    one = exchange(mine)
    held = pltpu.VMEM((blocks, slots, side, side), BF)
    agg, scaling = call(
        agg_kernel,
        "agg",
        [SMEM, SMEM, HBM, HBM],
        [((owners, feats, width), BF), ((blocks, side), F32)],
        [pltpu.VMEM((feats, nodes), BF), held, DMA((1,)), DMA((steps,))],
        flops=2 * 48 * 512 * 8192,
        size=9 << 20,
    )(tile_source, tile_count, node_features, edge_tiles)
    (send,) = call(
        back_kernel,
        "back",
        [SMEM, SMEM, VMEM, VMEM, HBM, VMEM],
        [((owners, rows, width), BF)],
        [pltpu.VMEM((blocks, cols, side), F32), held, DMA((steps,))],
        flops=2 * 16 * 512 * 8192,
        size=9 << 20,
    )(tile_source, tile_count, one, scaling, edge_tiles, agg)
    two = exchange(send)

    shifts = jnp.arange(32, dtype=jnp.int32)
    bits = jnp.bitwise_and(jnp.right_shift(drop_bits[:, :, None], shifts), 1)
    keep = (bits.reshape(drop_bits.shape[0], hidden_width).astype(F32) * 2.0).T
    core = (lax.axis_index("dp") % 2).reshape(1)
    wide = (hidden_width, width)
    pre, back = call(
        early_kernel, "early", [VMEM, VMEM, VMEM, VMEM], [(wide, F32), (wide, F32)], flops=400 << 20, size=4 << 20
    )(mine, one, self_first.T, self_second)
    gt = pltpu.VMEM((owners, cols, width), BF)
    send, hidden, d_pre = call(
        send_kernel,
        "send",
        [SMEM, HBM, VMEM, VMEM, HBM, HBM, VMEM, HBM, HBM],
        [((owners, rows, hidden_width), BF), (wide, BF), (wide, BF)],
        [
            gt,
            pltpu.VMEM(wide, F32),
            pltpu.VMEM(wide, F32),
            pltpu.VMEM((hidden_width, self_first.shape[0]), BF),
            pltpu.VMEM((hidden_width, hidden_width), BF),
            DMA((5,)),
        ],
        flops=800 << 20,
        size=6 << 20,
    )(core, mine, one, two, pre, back, keep, neigh_first.T, neigh_second)
    swap = [(i, i ^ 1) for i in range(replicas)]
    other = lax.ppermute(send, "dp", swap)
    (kept,) = call(
        keep_kernel,
        "keep",
        [SMEM, HBM, VMEM, VMEM, HBM, HBM],
        [((owners, rows, hidden_width), BF)],
        [gt, pltpu.VMEM(wide, BF), pltpu.VMEM(wide, BF), DMA((3,))],
        flops=400 << 20,
        size=3 << 20,
    )(core, mine, one, two, hidden, d_pre)

    xs, zs = 4, owners // 4
    x = lax.axis_index("feat") // zs

    def along_x(value, flip):
        return lax.ppermute(value, "feat", [(i, i ^ (flip * zs)) for i in range(owners)])

    by_x = (xs, zs, rows, hidden_width)
    two_slots = ((2, zs // 2, rows, hidden_width), BF)
    send_a, send_b, own_a, own_b = call(
        sum_one_kernel, "sum_one", [SMEM, VMEM, VMEM], [two_slots] * 4, size=4 << 20
    )(x.reshape(1), kept.reshape(by_x), other.reshape(by_x))
    got_a, got_b = along_x(send_a, 1), along_x(send_b, 3)
    one_slot = ((zs // 2, rows, hidden_width), BF)
    all_z = ((zs, rows, hidden_width), BF)
    send_a, send_b, own = call(sum_two_kernel, "sum_two", [VMEM] * 4, [one_slot, one_slot, all_z])(
        own_a, own_b, got_a, got_b
    )
    got_a, got_b = along_x(send_a, 3), along_x(send_b, 1)
    (own,) = call(sum_three_kernel, "sum_three", [VMEM] * 3, [all_z])(own, got_a, got_b)
    shares = exchange(own, axis_index_groups=[[a * zs + b for b in range(zs)] for a in range(xs)])
    share = jnp.sum(shares.astype(F32), axis=0).astype(BF)
    ys = replicas // 2
    total = share.astype(F32)
    for k in (1, 3, 2):
        to = [(i, ((i // 2 + k) % ys) * 2 + i % 2) for i in range(replicas)]
        total = total + lax.ppermute(share, "dp", to).astype(F32)
    return tuple(
        call(
            place_kernel,
            "place",
            [SMEM, VMEM, VMEM],
            [((r, hidden_width), F32) for r in (feats, feats, cols, cols)],
        )(core, total, lax.ppermute(total, "dp", swap))
    )


def solution(mesh):
    return jax.shard_map(
        functools.partial(local, owners=mesh.shape["feat"], replicas=mesh.shape["dp"]),
        mesh=mesh,
        in_specs=(
            P("feat", "dp"),
            P("dp", None, None, None),
            P("dp", None),
            P("dp"),
            P(("dp", "feat"), None),
            P(("dp", "feat"), None),
            P(),
            P(),
            P(),
            P(),
        ),
        out_specs=(P("feat", None), P("feat", None), P("feat", None), P("feat", None)),
        check_vma=False,
    )
```

```python
import functools

import jax
import jax.numpy as jnp
from jax import lax
from jax.experimental import pallas as pl
from jax.experimental.pallas import tpu as pltpu
from jax.sharding import PartitionSpec as P

BF = jnp.bfloat16
F32 = jnp.float32
STEP = 8
FEATS = 32
LAST = (((1,), (1,)), ((), ()))


def alive(count, slot):
    return jnp.where(slot < count, 1.0, 0.0).astype(F32)


def begin(pairs, sems):
    copies = [pltpu.make_async_copy(src, dst, sems.at[i]) for i, (src, dst) in enumerate(pairs)]
    for copy in copies:
        copy.start()
    return copies


def chunk(tiles_ref, held_ref, sems, i):
    part = pl.ds(i * STEP, STEP)
    return pltpu.make_async_copy(tiles_ref.at[part], held_ref.at[part], sems.at[i])


def prep_kernel(x_ref, g_ref, out_ref, x_held, g_held, sems):
    owners, rows, width = out_ref.shape
    copies = begin([(g_ref, g_held), (x_ref, x_held)], sems)
    copies[0].wait()
    out_ref[:, FEATS:, :] = g_held[...].T.reshape(owners, rows - FEATS, width)
    copies[1].wait()
    for o in range(owners):
        out_ref[o, :FEATS, :] = x_held[:, o * width : (o + 1) * width]


def agg_kernel(source_ref, count_ref, x_ref, tiles_ref, agg_ref, scale_ref, x_held, held_ref, x_sem, sems):
    blocks, slots, side, _ = held_ref.shape
    steps = blocks // STEP
    copies = begin([(x_ref, x_held)], x_sem)
    for i in range(steps):
        chunk(tiles_ref, held_ref, sems, i).start()
    copies[0].wait()

    @pl.loop(0, steps)
    def _(i):
        chunk(tiles_ref, held_ref, sems, i).wait()
        for j in range(STEP):
            b = i * STEP + j
            count = count_ref[b]
            parts = []
            for t in range(slots):
                start = pl.multiple_of(source_ref[b, t] * side, side)
                x = jnp.concatenate([x_held[:, pl.ds(start, side)], jnp.ones((16, side), BF)], axis=0)
                parts.append(x * jnp.full((FEATS + 16, side), alive(count, t), F32).astype(BF))
            lhs = jnp.concatenate(parts, axis=1)
            rhs = jnp.concatenate([held_ref[b, t] for t in range(slots)], axis=1)
            out = lax.dot_general(lhs, rhs, LAST, preferred_element_type=F32)
            scale = lax.rsqrt(out[FEATS : FEATS + 1])
            agg_ref[b // 2, :FEATS, (j % 2) * side : (j % 2 + 1) * side] = (out[:FEATS] * scale).astype(BF)
            scale_ref[pl.ds(b, 1)] = scale


def back_kernel(source_ref, count_ref, one_ref, scale_ref, tiles_ref, agg_ref, out_ref, acc_ref, q_ref, held_ref, sems, out_sem):
    blocks, slots, side, _ = held_ref.shape
    steps = blocks // STEP
    for i in range(steps):
        chunk(tiles_ref, held_ref, sems, i).start()
    acc_ref[...] = jnp.zeros_like(acc_ref)

    @pl.loop(0, steps)
    def _(i):
        chunk(tiles_ref, held_ref, sems, i).wait()
        for j in range(STEP):
            b = i * STEP + j
            count = count_ref[b]
            g = one_ref[b // 2, FEATS:, (j % 2) * side : (j % 2 + 1) * side].astype(F32)
            g = (g * scale_ref[pl.ds(b, 1)]).astype(BF)
            rhs = jnp.concatenate([held_ref[b, t] for t in range(slots)], axis=1)
            out = jnp.dot(g, rhs, preferred_element_type=F32)
            for t in range(slots):
                src = source_ref[b, t]
                acc_ref[src] = acc_ref[src] + out[:, t * side : (t + 1) * side] * alive(count, t)

    for o in range(q_ref.shape[0]):
        q_ref[o, :, :side] = acc_ref[2 * o].astype(BF)
        q_ref[o, :, side:] = acc_ref[2 * o + 1].astype(BF)
    begin([(q_ref, out_ref.at[:, FEATS:, :])], out_sem)[0].wait()


def upper(ref):
    owners, _, width = ref.shape
    return ref[:, :FEATS, :].reshape(owners * FEATS, width)


def lower(ref):
    owners, rows, width = ref.shape
    return ref[:, FEATS:, :].reshape(owners * (rows - FEATS), width)


def early_kernel(mine_ref, one_ref, wsf_ref, wss_ref, pre_ref, back_ref):
    pre_ref[...] = jnp.dot(wsf_ref[...], upper(one_ref), preferred_element_type=F32)
    back_ref[...] = jnp.dot(wss_ref[...], lower(mine_ref), preferred_element_type=F32)


def write_half(half, gt_ref, one_ref, two_ref, hidden, d_pre, out_ref):
    ys, owners, rows, lanes = out_ref.shape
    if half:
        left, right = upper(two_ref), lower(two_ref)
    else:
        left, right = upper(one_ref), gt_ref[...].reshape(hidden.shape)
    first = lax.dot_general(left, d_pre, LAST, preferred_element_type=F32).astype(BF)
    second = lax.dot_general(hidden, right, LAST, preferred_element_type=F32).astype(BF)
    for y in range(ys):
        cut = slice(y * lanes, (y + 1) * lanes)
        out_ref[y, :, :FEATS, :] = first[:, cut].reshape(owners, FEATS, lanes)
        out_ref[y, :, FEATS:, :] = second[:, cut].reshape(owners, rows - FEATS, lanes)


def send_kernel(
    core_ref,
    mine_ref,
    one_ref,
    two_ref,
    pre_ref,
    back_ref,
    keep_ref,
    wnf_ref,
    wns_ref,
    send_ref,
    hidden_out,
    d_pre_out,
    gt_held,
    pre_held,
    back_held,
    wnf_held,
    wns_held,
    hidden_ref,
    d_pre_ref,
    sems,
    out_sems,
):
    copies = begin(
        [
            (wnf_ref, wnf_held),
            (pre_ref, pre_held),
            (wns_ref, wns_held),
            (back_ref, back_held),
            (mine_ref.at[:, FEATS:, :], gt_held),
        ],
        sems,
    )
    copies[0].wait()
    pre = jnp.dot(wnf_held[...], upper(two_ref), preferred_element_type=F32)
    copies[1].wait()
    pre = pre + pre_held[...]
    hidden_width, width = pre.shape
    side = width // 2
    keep = jnp.concatenate(
        [
            jnp.broadcast_to(keep_ref[:, 0:1], (hidden_width, side)),
            jnp.broadcast_to(keep_ref[:, 1:2], (hidden_width, side)),
        ],
        axis=1,
    )
    sigma = jax.nn.sigmoid(pre)
    hidden_ref[...] = (pre * sigma * keep).astype(BF)
    slope = sigma * (1.0 + pre * (1.0 - sigma)) * keep
    copies[2].wait()
    back = jnp.dot(wns_held[...], lower(two_ref), preferred_element_type=F32)
    copies[3].wait()
    d_pre_ref[...] = ((back + back_held[...]) * slope).astype(BF)
    copies[4].wait()
    leaving = begin([(hidden_ref, hidden_out), (d_pre_ref, d_pre_out)], out_sems)
    for core in range(2):

        @pl.when(core_ref[0] == core)
        def _():
            write_half(1 - core, gt_held, one_ref, two_ref, hidden_ref[...], d_pre_ref[...], send_ref)

    for copy in leaving:
        copy.wait()


def keep_kernel(core_ref, mine_ref, one_ref, two_ref, hidden_ref, d_pre_ref, keep_ref, gt_held, hidden, d_pre, sems):
    copies = begin(
        [(d_pre_ref, d_pre), (hidden_ref, hidden), (mine_ref.at[:, FEATS:, :], gt_held)], sems
    )
    for copy in copies:
        copy.wait()
    for core in range(2):

        @pl.when(core_ref[0] == core)
        def _():
            write_half(core, gt_held, one_ref, two_ref, hidden[...], d_pre[...], keep_ref)


def pair_kernel(keep_ref, other_ref, out_ref):
    out_ref[...] = (keep_ref[...].astype(F32) + other_ref[...].astype(F32)).astype(BF)


def gather_kernel(got_ref, out_ref):
    total = got_ref[0].astype(F32)
    for i in range(1, got_ref.shape[0]):
        total = total + got_ref[i].astype(F32)
    out_ref[...] = total.astype(BF)


def place_kernel(where_ref, *refs):
    ins, outs = refs[:4], refs[4:]
    ys = len(ins)
    for core in range(2):

        @pl.when(where_ref[0] == core)
        def _():
            for k in range(ys):
                start = pl.multiple_of(lax.rem(where_ref[1] + ys - k, ys) * 128, 128)
                for r in range(2):
                    half = core ^ r
                    outs[half][:, pl.ds(start, 128)] = ins[k][r, :FEATS]
                    outs[2 + half][:, pl.ds(start, 128)] = ins[k][r, FEATS:]


SMEM = pl.BlockSpec(memory_space=pltpu.SMEM)
VMEM = pl.BlockSpec(memory_space=pltpu.VMEM)
HBM = pl.BlockSpec(memory_space=pltpu.HBM)
DMA = pltpu.SemaphoreType.DMA


def call(kernel, name, ins, outs, scratch=(), flops=0, size=1 << 20, aliases=None):
    run = pl.pallas_call(
        kernel,
        in_specs=list(ins),
        out_specs=[HBM if len(o) > 2 else VMEM for o in outs],
        out_shape=[(pltpu.HBM if len(o) > 2 else jax.ShapeDtypeStruct)(*o[:2]) for o in outs],
        scratch_shapes=list(scratch),
        input_output_aliases=aliases or {},
        compiler_params=pltpu.CompilerParams(vmem_limit_bytes=24 << 20),
        cost_estimate=pl.CostEstimate(flops=flops, bytes_accessed=size, transcendentals=0),
        name=name,
    )

    def apply(*args):
        return run(
            *(
                pltpu.with_memory_space_constraint(a, pltpu.HBM) if spec is HBM else a
                for a, spec in zip(args, ins, strict=True)
            )
        )

    return apply


def local(
    node_features,
    edge_tiles,
    tile_source,
    tile_count,
    drop_bits,
    cotangent,
    self_first,
    neigh_first,
    self_second,
    neigh_second,
    owners,
    replicas,
):
    blocks, slots, side, _ = edge_tiles.shape
    feats, nodes = node_features.shape
    width = nodes // owners
    hidden_width = self_first.shape[1]
    cols = hidden_width // owners
    rows = feats + cols
    steps = blocks // STEP
    exchange = functools.partial(lax.all_to_all, axis_name="feat", split_axis=0, concat_axis=0, tiled=True)

    (mine,) = call(
        prep_kernel,
        "prep",
        [HBM] * 2,
        [((owners, rows, width), BF)],
        [pltpu.VMEM((feats, nodes), BF), pltpu.VMEM((width, hidden_width), BF), DMA((2,))],
    )(node_features, cotangent)
    one = exchange(mine)
    held = pltpu.VMEM((blocks, slots, side, side), BF)
    agg, scaling = call(
        agg_kernel,
        "agg",
        [SMEM, SMEM, HBM, HBM],
        [((owners, rows, width), BF), ((blocks, side), F32)],
        [pltpu.VMEM((feats, nodes), BF), held, DMA((1,)), DMA((steps,))],
        flops=2 * 48 * 512 * 8192,
        size=9 << 20,
    )(tile_source, tile_count, node_features, edge_tiles)
    (send,) = call(
        back_kernel,
        "back",
        [SMEM, SMEM, VMEM, VMEM, HBM, HBM],
        [((owners, rows, width), BF, HBM)],
        [pltpu.VMEM((blocks, cols, side), F32), pltpu.VMEM((owners, cols, width), BF), held, DMA((steps,)), DMA((1,))],
        flops=2 * 16 * 512 * 8192,
        size=9 << 20,
        aliases={5: 0},
    )(tile_source, tile_count, one, scaling, edge_tiles, agg)
    two = exchange(send)

    shifts = jnp.arange(32, dtype=jnp.int32)
    bits = jnp.bitwise_and(jnp.right_shift(drop_bits[:, :, None], shifts), 1)
    keep = (bits.reshape(drop_bits.shape[0], hidden_width).astype(F32) * 2.0).T
    core = (lax.axis_index("dp") % 2).reshape(1)
    wide = (hidden_width, width)
    pre, back = call(
        early_kernel, "early", [VMEM, VMEM, VMEM, VMEM], [(wide, F32), (wide, F32)], flops=400 << 20, size=4 << 20
    )(mine, one, self_first.T, self_second)
    gt = pltpu.VMEM((owners, cols, width), BF)
    ys, xs = replicas // 2, 4
    zs = owners // xs
    half = ((ys, owners, rows, 128), BF)
    send, hidden, d_pre = call(
        send_kernel,
        "send",
        [SMEM, HBM, VMEM, VMEM, HBM, HBM, VMEM, HBM, HBM],
        [half, (wide, BF, HBM), (wide, BF, HBM)],
        [
            gt,
            pltpu.VMEM(wide, F32),
            pltpu.VMEM(wide, F32),
            pltpu.VMEM((hidden_width, self_first.shape[0]), BF),
            pltpu.VMEM((hidden_width, hidden_width), BF),
            pltpu.VMEM(wide, BF),
            pltpu.VMEM(wide, BF),
            DMA((5,)),
            DMA((2,)),
        ],
        flops=800 << 20,
        size=6 << 20,
    )(core, mine, one, two, pre, back, keep, neigh_first.T, neigh_second)
    swap = [(i, i ^ 1) for i in range(replicas)]
    other = lax.ppermute(send, "dp", swap)
    (kept,) = call(
        keep_kernel,
        "keep",
        [SMEM, HBM, VMEM, VMEM, HBM, HBM],
        [half],
        [gt, pltpu.VMEM(wide, BF), pltpu.VMEM(wide, BF), DMA((3,))],
        flops=400 << 20,
        size=3 << 20,
    )(core, mine, one, two, hidden, d_pre)

    (pair,) = call(pair_kernel, "pair", [VMEM] * 2, [half], size=5 << 20)(kept, other)
    planes = [
        [(2 * y + c) * owners + x * zs + z for y in range(ys) for x in range(xs)] for c in range(2) for z in range(zs)
    ]
    got = lax.all_to_all(
        pair.reshape(ys * xs, zs, rows, 128), ("dp", "feat"), 0, 0, tiled=True, axis_index_groups=planes
    )
    (own,) = call(gather_kernel, "gather", [VMEM], [((zs, rows, 128), BF)], size=2 << 20)(got)
    shares = exchange(own, axis_index_groups=[[a * zs + b for b in range(zs)] for a in range(xs)])
    share = jnp.sum(shares.astype(F32), axis=0)
    both = jnp.stack([share, lax.ppermute(share, "dp", swap)])
    moved = {0: both}
    for k in (1, 3, 2):
        moved[k] = lax.ppermute(both, "dp", [(i, ((i // 2 + k) % ys) * 2 + i % 2) for i in range(replicas)])
    where = jnp.concatenate([core, (lax.axis_index("dp") // 2).reshape(1)])
    return tuple(
        call(
            place_kernel,
            "place",
            [SMEM] + [VMEM] * ys,
            [((r, hidden_width), F32) for r in (feats, feats, cols, cols)],
        )(where, *(moved[k] for k in range(ys)))
    )


def solution(mesh):
    return jax.shard_map(
        functools.partial(local, owners=mesh.shape["feat"], replicas=mesh.shape["dp"]),
        mesh=mesh,
        in_specs=(
            P("feat", "dp"),
            P("dp", None, None, None),
            P("dp", None),
            P("dp"),
            P(("dp", "feat"), None),
            P(("dp", "feat"), None),
            P(),
            P(),
            P(),
            P(),
        ),
        out_specs=(P("feat", None), P("feat", None), P("feat", None), P("feat", None)),
        check_vma=False,
    )
```

```python
import functools

import jax
import jax.numpy as jnp
from jax import lax
from jax.experimental import pallas as pl
from jax.experimental.pallas import tpu as pltpu
from jax.sharding import PartitionSpec as P

BF = jnp.bfloat16
F32 = jnp.float32
STEP = 8
FRONT = 16
FEATS = 32
LAST = (((1,), (1,)), ((), ()))


def alive(count, slot):
    return jnp.where(slot < count, 1.0, 0.0).astype(F32)


def begin(pairs, sems):
    copies = [pltpu.make_async_copy(src, dst, sems.at[i]) for i, (src, dst) in enumerate(pairs)]
    for copy in copies:
        copy.start()
    return copies


def chunk(tiles_ref, held_ref, sems, i):
    part = pl.ds(i * STEP, STEP)
    return pltpu.make_async_copy(tiles_ref.at[part], held_ref.at[part], sems.at[i])


def prep_kernel(x_ref, g_ref, out_ref, x_held, g_held, sems):
    owners, rows, width = out_ref.shape
    copies = begin([(g_ref, g_held), (x_ref, x_held)], sems)
    copies[0].wait()
    out_ref[:, FEATS:, :] = g_held[...].T.reshape(owners, rows - FEATS, width)
    copies[1].wait()
    for o in range(owners):
        out_ref[o, :FEATS, :] = x_held[:, o * width : (o + 1) * width]


def agg_kernel(source_ref, count_ref, x_ref, tiles_ref, agg_ref, scale_ref, front_ref, x_held, held_ref, x_sem, sems):
    blocks, slots, side, _ = held_ref.shape
    steps = blocks // STEP
    copies = begin([(x_ref, x_held)], x_sem)
    for i in range(steps):
        chunk(tiles_ref, held_ref, sems, i).start()
    copies[0].wait()

    @pl.loop(0, steps)
    def _(i):
        chunk(tiles_ref, held_ref, sems, i).wait()
        for j in range(STEP):
            b = i * STEP + j
            count = count_ref[b]
            parts = []
            for t in range(slots):
                start = pl.multiple_of(source_ref[b, t] * side, side)
                x = jnp.concatenate([x_held[:, pl.ds(start, side)], jnp.ones((16, side), BF)], axis=0)
                parts.append(x * jnp.full((FEATS + 16, side), alive(count, t), F32).astype(BF))
            lhs = jnp.concatenate(parts, axis=1)
            rhs = jnp.concatenate([held_ref[b, t] for t in range(slots)], axis=1)
            out = lax.dot_general(lhs, rhs, LAST, preferred_element_type=F32)
            scale = lax.rsqrt(out[FEATS : FEATS + 1])
            agg_ref[b // 2, :FEATS, (j % 2) * side : (j % 2 + 1) * side] = (out[:FEATS] * scale).astype(BF)
            scale_ref[pl.ds(b, 1)] = scale

    front_ref[...] = held_ref[: front_ref.shape[0]]


def back_kernel(
    source_ref, count_ref, one_ref, scale_ref, tiles_ref, front_ref, agg_ref, out_ref, acc_ref, q_ref, held_ref, sems, out_sem
):
    blocks, slots, side, _ = held_ref.shape
    steps, first = blocks // STEP, front_ref.shape[0] // STEP
    for i in range(first, steps):
        chunk(tiles_ref, held_ref, sems, i).start()
    acc_ref[...] = jnp.zeros_like(acc_ref)

    def add_up(i, tiles):
        for j in range(STEP):
            b = i * STEP + j
            count = count_ref[b]
            g = one_ref[b // 2, FEATS:, (j % 2) * side : (j % 2 + 1) * side].astype(F32)
            g = (g * scale_ref[pl.ds(b, 1)]).astype(BF)
            rhs = jnp.concatenate([tiles[b, t] for t in range(slots)], axis=1)
            out = jnp.dot(g, rhs, preferred_element_type=F32)
            for t in range(slots):
                src = source_ref[b, t]
                acc_ref[src] = acc_ref[src] + out[:, t * side : (t + 1) * side] * alive(count, t)

    @pl.loop(0, first)
    def _(i):
        add_up(i, front_ref)

    @pl.loop(first, steps)
    def _(i):
        chunk(tiles_ref, held_ref, sems, i).wait()
        add_up(i, held_ref)

    for o in range(q_ref.shape[0]):
        q_ref[o, :, :side] = acc_ref[2 * o].astype(BF)
        q_ref[o, :, side:] = acc_ref[2 * o + 1].astype(BF)
    begin([(q_ref, out_ref.at[:, FEATS:, :])], out_sem)[0].wait()


def upper(ref):
    owners, _, width = ref.shape
    return ref[:, :FEATS, :].reshape(owners * FEATS, width)


def lower(ref):
    owners, rows, width = ref.shape
    return ref[:, FEATS:, :].reshape(owners * (rows - FEATS), width)


def early_kernel(mine_ref, one_ref, wsf_ref, wss_ref, pre_ref, back_ref):
    pre_ref[...] = jnp.dot(wsf_ref[...], upper(one_ref), preferred_element_type=F32)
    back_ref[...] = jnp.dot(wss_ref[...], lower(mine_ref), preferred_element_type=F32)


def write_half(half, gt_ref, one_ref, two_ref, hidden, d_pre, out_ref):
    ys, owners, rows, lanes = out_ref.shape
    if half:
        left, right = upper(two_ref), lower(two_ref)
    else:
        left, right = upper(one_ref), gt_ref[...].reshape(hidden.shape)
    first = lax.dot_general(left, d_pre, LAST, preferred_element_type=F32).astype(BF)
    second = lax.dot_general(hidden, right, LAST, preferred_element_type=F32).astype(BF)
    for y in range(ys):
        cut = slice(y * lanes, (y + 1) * lanes)
        out_ref[y, :, :FEATS, :] = first[:, cut].reshape(owners, FEATS, lanes)
        out_ref[y, :, FEATS:, :] = second[:, cut].reshape(owners, rows - FEATS, lanes)


def send_kernel(
    core_ref,
    mine_ref,
    one_ref,
    two_ref,
    pre_ref,
    back_ref,
    keep_ref,
    wnf_ref,
    wns_ref,
    send_ref,
    hidden_out,
    d_pre_out,
    gt_held,
    pre_held,
    back_held,
    wnf_held,
    wns_held,
    hidden_ref,
    d_pre_ref,
    sems,
    out_sems,
):
    copies = begin(
        [
            (wnf_ref, wnf_held),
            (pre_ref, pre_held),
            (wns_ref, wns_held),
            (back_ref, back_held),
            (mine_ref.at[:, FEATS:, :], gt_held),
        ],
        sems,
    )
    copies[0].wait()
    pre = jnp.dot(wnf_held[...], upper(two_ref), preferred_element_type=F32)
    copies[1].wait()
    pre = pre + pre_held[...]
    hidden_width, width = pre.shape
    side = width // 2
    keep = jnp.concatenate(
        [
            jnp.broadcast_to(keep_ref[:, 0:1], (hidden_width, side)),
            jnp.broadcast_to(keep_ref[:, 1:2], (hidden_width, side)),
        ],
        axis=1,
    )
    sigma = jax.nn.sigmoid(pre)
    hidden_ref[...] = (pre * sigma * keep).astype(BF)
    slope = sigma * (1.0 + pre * (1.0 - sigma)) * keep
    copies[2].wait()
    back = jnp.dot(wns_held[...], lower(two_ref), preferred_element_type=F32)
    copies[3].wait()
    d_pre_ref[...] = ((back + back_held[...]) * slope).astype(BF)
    copies[4].wait()
    leaving = begin([(hidden_ref, hidden_out), (d_pre_ref, d_pre_out)], out_sems)
    for core in range(2):

        @pl.when(core_ref[0] == core)
        def _():
            write_half(1 - core, gt_held, one_ref, two_ref, hidden_ref[...], d_pre_ref[...], send_ref)

    for copy in leaving:
        copy.wait()


def keep_kernel(core_ref, mine_ref, one_ref, two_ref, hidden_ref, d_pre_ref, keep_ref, gt_held, hidden, d_pre, sems):
    copies = begin(
        [(d_pre_ref, d_pre), (hidden_ref, hidden), (mine_ref.at[:, FEATS:, :], gt_held)], sems
    )
    for copy in copies:
        copy.wait()
    for core in range(2):

        @pl.when(core_ref[0] == core)
        def _():
            write_half(core, gt_held, one_ref, two_ref, hidden[...], d_pre[...], keep_ref)


def pair_kernel(keep_ref, other_ref, out_ref):
    out_ref[...] = (keep_ref[...].astype(F32) + other_ref[...].astype(F32)).astype(BF)


def gather_kernel(got_ref, out_ref):
    total = got_ref[0].astype(F32)
    for i in range(1, got_ref.shape[0]):
        total = total + got_ref[i].astype(F32)
    out_ref[...] = total.astype(BF)


def place_kernel(where_ref, *refs):
    ins, outs = refs[:4], refs[4:]
    ys = len(ins)
    for core in range(2):

        @pl.when(where_ref[0] == core)
        def _():
            for k in range(ys):
                start = pl.multiple_of(lax.rem(where_ref[1] + ys - k, ys) * 128, 128)
                for r in range(2):
                    half = core ^ r
                    outs[half][:, pl.ds(start, 128)] = ins[k][r, :FEATS]
                    outs[2 + half][:, pl.ds(start, 128)] = ins[k][r, FEATS:]


SMEM = pl.BlockSpec(memory_space=pltpu.SMEM)
VMEM = pl.BlockSpec(memory_space=pltpu.VMEM)
HBM = pl.BlockSpec(memory_space=pltpu.HBM)
DMA = pltpu.SemaphoreType.DMA


def call(kernel, name, ins, outs, scratch=(), flops=0, size=1 << 20, aliases=None):
    run = pl.pallas_call(
        kernel,
        in_specs=list(ins),
        out_specs=[o[2] if len(o) > 2 else VMEM for o in outs],
        out_shape=[
            ((pltpu.HBM if o[2] is HBM else pltpu.VMEM) if len(o) > 2 else jax.ShapeDtypeStruct)(*o[:2]) for o in outs
        ],
        scratch_shapes=list(scratch),
        input_output_aliases=aliases or {},
        compiler_params=pltpu.CompilerParams(vmem_limit_bytes=24 << 20),
        cost_estimate=pl.CostEstimate(flops=flops, bytes_accessed=size, transcendentals=0),
        name=name,
    )

    def apply(*args):
        return run(
            *(
                pltpu.with_memory_space_constraint(a, pltpu.HBM) if spec is HBM else a
                for a, spec in zip(args, ins, strict=True)
            )
        )

    return apply


def local(
    node_features,
    edge_tiles,
    tile_source,
    tile_count,
    drop_bits,
    cotangent,
    self_first,
    neigh_first,
    self_second,
    neigh_second,
    owners,
    replicas,
):
    blocks, slots, side, _ = edge_tiles.shape
    feats, nodes = node_features.shape
    width = nodes // owners
    hidden_width = self_first.shape[1]
    cols = hidden_width // owners
    rows = feats + cols
    steps = blocks // STEP
    exchange = functools.partial(lax.all_to_all, axis_name="feat", split_axis=0, concat_axis=0, tiled=True)

    (mine,) = call(
        prep_kernel,
        "prep",
        [HBM] * 2,
        [((owners, rows, width), BF)],
        [pltpu.VMEM((feats, nodes), BF), pltpu.VMEM((width, hidden_width), BF), DMA((2,))],
    )(node_features, cotangent)
    one = exchange(mine)
    held = pltpu.VMEM((blocks, slots, side, side), BF)
    agg, scaling, front = call(
        agg_kernel,
        "agg",
        [SMEM, SMEM, HBM, HBM],
        [((owners, rows, width), BF), ((blocks, side), F32), ((FRONT,) + edge_tiles.shape[1:], BF, VMEM)],
        [pltpu.VMEM((feats, nodes), BF), held, DMA((1,)), DMA((steps,))],
        flops=2 * 48 * 512 * 8192,
        size=9 << 20,
    )(tile_source, tile_count, node_features, edge_tiles)
    (send,) = call(
        back_kernel,
        "back",
        [SMEM, SMEM, VMEM, VMEM, HBM, VMEM, HBM],
        [((owners, rows, width), BF, HBM)],
        [pltpu.VMEM((blocks, cols, side), F32), pltpu.VMEM((owners, cols, width), BF), held, DMA((steps,)), DMA((1,))],
        flops=2 * 16 * 512 * 8192,
        size=9 << 20,
        aliases={6: 0},
    )(tile_source, tile_count, one, scaling, edge_tiles, front, agg)
    two = exchange(send)

    shifts = jnp.arange(32, dtype=jnp.int32)
    bits = jnp.bitwise_and(jnp.right_shift(drop_bits[:, :, None], shifts), 1)
    keep = (bits.reshape(drop_bits.shape[0], hidden_width).astype(F32) * 2.0).T
    core = (lax.axis_index("dp") % 2).reshape(1)
    wide = (hidden_width, width)
    pre, back = call(
        early_kernel, "early", [VMEM, VMEM, VMEM, VMEM], [(wide, F32), (wide, F32)], flops=400 << 20, size=4 << 20
    )(mine, one, self_first.T, self_second)
    gt = pltpu.VMEM((owners, cols, width), BF)
    ys, xs = replicas // 2, 4
    zs = owners // xs
    half = ((ys, owners, rows, 128), BF)
    send, hidden, d_pre = call(
        send_kernel,
        "send",
        [SMEM, HBM, VMEM, VMEM, HBM, HBM, VMEM, HBM, HBM],
        [half, (wide, BF, HBM), (wide, BF, HBM)],
        [
            gt,
            pltpu.VMEM(wide, F32),
            pltpu.VMEM(wide, F32),
            pltpu.VMEM((hidden_width, self_first.shape[0]), BF),
            pltpu.VMEM((hidden_width, hidden_width), BF),
            pltpu.VMEM(wide, BF),
            pltpu.VMEM(wide, BF),
            DMA((5,)),
            DMA((2,)),
        ],
        flops=800 << 20,
        size=6 << 20,
    )(core, mine, one, two, pre, back, keep, neigh_first.T, neigh_second)
    swap = [(i, i ^ 1) for i in range(replicas)]
    other = lax.ppermute(send, "dp", swap)
    (kept,) = call(
        keep_kernel,
        "keep",
        [SMEM, HBM, VMEM, VMEM, HBM, HBM],
        [half],
        [gt, pltpu.VMEM(wide, BF), pltpu.VMEM(wide, BF), DMA((3,))],
        flops=400 << 20,
        size=3 << 20,
    )(core, mine, one, two, hidden, d_pre)

    (pair,) = call(pair_kernel, "pair", [VMEM] * 2, [half], size=5 << 20)(kept, other)
    planes = [
        [(2 * y + c) * owners + x * zs + z for y in range(ys) for x in range(xs)] for c in range(2) for z in range(zs)
    ]
    got = lax.all_to_all(
        pair.reshape(ys * xs, zs, rows, 128), ("dp", "feat"), 0, 0, tiled=True, axis_index_groups=planes
    )
    (own,) = call(gather_kernel, "gather", [VMEM], [((zs, rows, 128), BF)], size=2 << 20)(got)
    shares = exchange(own, axis_index_groups=[[a * zs + b for b in range(zs)] for a in range(xs)])
    share = jnp.sum(shares.astype(F32), axis=0)
    both = jnp.stack([share, lax.ppermute(share, "dp", swap)])
    moved = {0: both}
    for k in (1, 3, 2):
        moved[k] = lax.ppermute(both, "dp", [(i, ((i // 2 + k) % ys) * 2 + i % 2) for i in range(replicas)])
    where = jnp.concatenate([core, (lax.axis_index("dp") // 2).reshape(1)])
    return tuple(
        call(
            place_kernel,
            "place",
            [SMEM] + [VMEM] * ys,
            [((r, hidden_width), F32) for r in (feats, feats, cols, cols)],
        )(where, *(moved[k] for k in range(ys)))
    )


def solution(mesh):
    return jax.shard_map(
        functools.partial(local, owners=mesh.shape["feat"], replicas=mesh.shape["dp"]),
        mesh=mesh,
        in_specs=(
            P("feat", "dp"),
            P("dp", None, None, None),
            P("dp", None),
            P("dp"),
            P(("dp", "feat"), None),
            P(("dp", "feat"), None),
            P(),
            P(),
            P(),
            P(),
        ),
        out_specs=(P("feat", None), P("feat", None), P("feat", None), P("feat", None)),
        check_vma=False,
    )
```

```python
import functools

import jax
import jax.numpy as jnp
from jax import lax
from jax.experimental import pallas as pl
from jax.experimental.pallas import tpu as pltpu
from jax.sharding import PartitionSpec as P

BF = jnp.bfloat16
F32 = jnp.float32
STEP = 8
FRONT = 16
FEATS = 32
LAST = (((1,), (1,)), ((), ()))


def alive(count, slot):
    return jnp.where(slot < count, 1.0, 0.0).astype(F32)


def begin(pairs, sems):
    copies = [pltpu.make_async_copy(src, dst, sems.at[i]) for i, (src, dst) in enumerate(pairs)]
    for copy in copies:
        copy.start()
    return copies


def chunk(tiles_ref, held_ref, sems, i):
    part = pl.ds(i * STEP, STEP)
    return pltpu.make_async_copy(tiles_ref.at[part], held_ref.at[part], sems.at[i])


def prep_kernel(x_ref, g_ref, out_ref, x_held, g_held, sems):
    owners, rows, width = out_ref.shape
    copies = begin([(g_ref, g_held), (x_ref, x_held)], sems)
    copies[0].wait()
    out_ref[:, FEATS:, :] = g_held[...].T.reshape(owners, rows - FEATS, width)
    copies[1].wait()
    for o in range(owners):
        out_ref[o, :FEATS, :] = x_held[:, o * width : (o + 1) * width]


def agg_kernel(source_ref, count_ref, x_ref, tiles_ref, agg_ref, scale_ref, front_ref, x_held, held_ref, x_sem, sems):
    blocks, slots, side, _ = held_ref.shape
    steps = blocks // STEP
    copies = begin([(x_ref, x_held)], x_sem)
    for i in range(steps):
        chunk(tiles_ref, held_ref, sems, i).start()
    copies[0].wait()

    @pl.loop(0, steps)
    def _(i):
        chunk(tiles_ref, held_ref, sems, i).wait()
        for j in range(STEP):
            b = i * STEP + j
            count = count_ref[b]
            parts = []
            for t in range(slots):
                start = pl.multiple_of(source_ref[b, t] * side, side)
                x = jnp.concatenate([x_held[:, pl.ds(start, side)], jnp.ones((16, side), BF)], axis=0)
                parts.append(x * jnp.full((FEATS + 16, side), alive(count, t), F32).astype(BF))
            lhs = jnp.concatenate(parts, axis=1)
            rhs = jnp.concatenate([held_ref[b, t] for t in range(slots)], axis=1)
            out = lax.dot_general(lhs, rhs, LAST, preferred_element_type=F32)
            scale = lax.rsqrt(out[FEATS : FEATS + 1])
            agg_ref[b // 2, :FEATS, (j % 2) * side : (j % 2 + 1) * side] = (out[:FEATS] * scale).astype(BF)
            scale_ref[pl.ds(b, 1)] = scale

    front_ref[...] = held_ref[: front_ref.shape[0]]


def back_kernel(
    source_ref, count_ref, one_ref, scale_ref, tiles_ref, front_ref, agg_ref, out_ref, acc_ref, q_ref, held_ref, sems, out_sem
):
    blocks, slots, side, _ = held_ref.shape
    steps, first = blocks // STEP, front_ref.shape[0] // STEP
    for i in range(first, steps):
        chunk(tiles_ref, held_ref, sems, i).start()
    acc_ref[...] = jnp.zeros_like(acc_ref)

    def add_up(i, tiles):
        for j in range(STEP):
            b = i * STEP + j
            count = count_ref[b]
            g = one_ref[b // 2, FEATS:, (j % 2) * side : (j % 2 + 1) * side].astype(F32)
            g = (g * scale_ref[pl.ds(b, 1)]).astype(BF)
            rhs = jnp.concatenate([tiles[b, t] for t in range(slots)], axis=1)
            out = jnp.dot(g, rhs, preferred_element_type=F32)
            for t in range(slots):
                src = source_ref[b, t]
                acc_ref[src] = acc_ref[src] + out[:, t * side : (t + 1) * side] * alive(count, t)

    @pl.loop(0, first)
    def _(i):
        add_up(i, front_ref)

    @pl.loop(first, steps)
    def _(i):
        chunk(tiles_ref, held_ref, sems, i).wait()
        add_up(i, held_ref)

    for o in range(q_ref.shape[0]):
        q_ref[o, :, :side] = acc_ref[2 * o].astype(BF)
        q_ref[o, :, side:] = acc_ref[2 * o + 1].astype(BF)
    begin([(q_ref, out_ref.at[:, FEATS:, :])], out_sem)[0].wait()


def upper(ref):
    owners, _, width = ref.shape
    return ref[:, :FEATS, :].reshape(owners * FEATS, width)


def lower(ref):
    owners, rows, width = ref.shape
    return ref[:, FEATS:, :].reshape(owners * (rows - FEATS), width)


def early_kernel(mine_ref, one_ref, wsf_ref, wss_ref, pre_ref, back_ref):
    pre_ref[...] = jnp.dot(wsf_ref[...], upper(one_ref), preferred_element_type=F32)
    back_ref[...] = jnp.dot(wss_ref[...], lower(mine_ref), preferred_element_type=F32)


def write_half(half, gt_ref, one_ref, two_ref, hidden, d_pre, out_ref):
    ys, owners, rows, lanes = out_ref.shape
    if half:
        left, right = upper(two_ref), lower(two_ref)
    else:
        left, right = upper(one_ref), gt_ref[...].reshape(hidden.shape)
    first = lax.dot_general(left, d_pre, LAST, preferred_element_type=F32).astype(BF)
    second = lax.dot_general(hidden, right, LAST, preferred_element_type=F32).astype(BF)
    for y in range(ys):
        cut = slice(y * lanes, (y + 1) * lanes)
        out_ref[y, :, :FEATS, :] = first[:, cut].reshape(owners, FEATS, lanes)
        out_ref[y, :, FEATS:, :] = second[:, cut].reshape(owners, rows - FEATS, lanes)


def send_kernel(
    core_ref,
    mine_ref,
    one_ref,
    two_ref,
    pre_ref,
    back_ref,
    keep_ref,
    wnf_ref,
    wns_ref,
    send_ref,
    hidden_out,
    d_pre_out,
    gt_held,
    pre_held,
    back_held,
    wnf_held,
    wns_held,
    hidden_ref,
    d_pre_ref,
    sems,
    out_sems,
):
    copies = begin(
        [
            (wnf_ref, wnf_held),
            (pre_ref, pre_held),
            (wns_ref, wns_held),
            (back_ref, back_held),
            (mine_ref.at[:, FEATS:, :], gt_held),
        ],
        sems,
    )
    copies[0].wait()
    pre = jnp.dot(wnf_held[...], upper(two_ref), preferred_element_type=F32)
    copies[1].wait()
    pre = pre + pre_held[...]
    hidden_width, width = pre.shape
    side = width // 2
    keep = jnp.concatenate(
        [
            jnp.broadcast_to(keep_ref[:, 0:1], (hidden_width, side)),
            jnp.broadcast_to(keep_ref[:, 1:2], (hidden_width, side)),
        ],
        axis=1,
    )
    sigma = jax.nn.sigmoid(pre)
    hidden_ref[...] = (pre * sigma * keep).astype(BF)
    slope = sigma * (1.0 + pre * (1.0 - sigma)) * keep
    copies[2].wait()
    back = jnp.dot(wns_held[...], lower(two_ref), preferred_element_type=F32)
    copies[3].wait()
    d_pre_ref[...] = ((back + back_held[...]) * slope).astype(BF)
    copies[4].wait()
    leaving = begin([(hidden_ref, hidden_out), (d_pre_ref, d_pre_out)], out_sems)
    for core in range(2):

        @pl.when(core_ref[0] == core)
        def _():
            write_half(1 - core, gt_held, one_ref, two_ref, hidden_ref[...], d_pre_ref[...], send_ref)

    for copy in leaving:
        copy.wait()


def keep_kernel(core_ref, mine_ref, one_ref, two_ref, hidden_ref, d_pre_ref, keep_ref, gt_held, hidden, d_pre, sems):
    copies = begin(
        [(d_pre_ref, d_pre), (hidden_ref, hidden), (mine_ref.at[:, FEATS:, :], gt_held)], sems
    )
    for copy in copies:
        copy.wait()
    for core in range(2):

        @pl.when(core_ref[0] == core)
        def _():
            write_half(core, gt_held, one_ref, two_ref, hidden[...], d_pre[...], keep_ref)


def add(*terms):
    total = terms[0].astype(F32)
    for term in terms[1:]:
        total = total + term.astype(F32)
    return total.astype(BF)


def pair_kernel(slot_ref, keep_ref, other_ref, *outs):
    for i, out in enumerate(outs):
        for j in range(4):
            slot = slot_ref[4 * i + j]
            out[j] = add(keep_ref[slot], other_ref[slot])


def square_kernel(own_ref, got_one, got_two, got_three, out_ref):
    out_ref[...] = add(own_ref[...], got_one[...], got_two[...], got_three[...])


def place_kernel(where_ref, *refs):
    ins, outs = refs[:4], refs[4:]
    ys = len(ins)
    for core in range(2):

        @pl.when(where_ref[0] == core)
        def _():
            for k in range(ys):
                start = pl.multiple_of(lax.rem(where_ref[1] + ys - k, ys) * 128, 128)
                for r in range(2):
                    half = core ^ r
                    outs[half][:, pl.ds(start, 128)] = ins[k][r, :FEATS]
                    outs[2 + half][:, pl.ds(start, 128)] = ins[k][r, FEATS:]


SMEM = pl.BlockSpec(memory_space=pltpu.SMEM)
VMEM = pl.BlockSpec(memory_space=pltpu.VMEM)
HBM = pl.BlockSpec(memory_space=pltpu.HBM)
DMA = pltpu.SemaphoreType.DMA


def call(kernel, name, ins, outs, scratch=(), flops=0, size=1 << 20, aliases=None):
    run = pl.pallas_call(
        kernel,
        in_specs=list(ins),
        out_specs=[o[2] if len(o) > 2 else VMEM for o in outs],
        out_shape=[
            ((pltpu.HBM if o[2] is HBM else pltpu.VMEM) if len(o) > 2 else jax.ShapeDtypeStruct)(*o[:2]) for o in outs
        ],
        scratch_shapes=list(scratch),
        input_output_aliases=aliases or {},
        compiler_params=pltpu.CompilerParams(vmem_limit_bytes=24 << 20),
        cost_estimate=pl.CostEstimate(flops=flops, bytes_accessed=size, transcendentals=0),
        name=name,
    )

    def apply(*args):
        return run(
            *(
                pltpu.with_memory_space_constraint(a, pltpu.HBM) if spec is HBM else a
                for a, spec in zip(args, ins, strict=True)
            )
        )

    return apply


def local(
    node_features,
    edge_tiles,
    tile_source,
    tile_count,
    drop_bits,
    cotangent,
    self_first,
    neigh_first,
    self_second,
    neigh_second,
    owners,
    replicas,
):
    blocks, slots, side, _ = edge_tiles.shape
    feats, nodes = node_features.shape
    width = nodes // owners
    hidden_width = self_first.shape[1]
    cols = hidden_width // owners
    rows = feats + cols
    steps = blocks // STEP
    exchange = functools.partial(lax.all_to_all, axis_name="feat", split_axis=0, concat_axis=0, tiled=True)

    (mine,) = call(
        prep_kernel,
        "prep",
        [HBM] * 2,
        [((owners, rows, width), BF)],
        [pltpu.VMEM((feats, nodes), BF), pltpu.VMEM((width, hidden_width), BF), DMA((2,))],
    )(node_features, cotangent)
    one = exchange(mine)
    held = pltpu.VMEM((blocks, slots, side, side), BF)
    agg, scaling, front = call(
        agg_kernel,
        "agg",
        [SMEM, SMEM, HBM, HBM],
        [((owners, rows, width), BF), ((blocks, side), F32), ((FRONT,) + edge_tiles.shape[1:], BF, VMEM)],
        [pltpu.VMEM((feats, nodes), BF), held, DMA((1,)), DMA((steps,))],
        flops=2 * 48 * 512 * 8192,
        size=9 << 20,
    )(tile_source, tile_count, node_features, edge_tiles)
    (send,) = call(
        back_kernel,
        "back",
        [SMEM, SMEM, VMEM, VMEM, HBM, VMEM, HBM],
        [((owners, rows, width), BF, HBM)],
        [pltpu.VMEM((blocks, cols, side), F32), pltpu.VMEM((owners, cols, width), BF), held, DMA((steps,)), DMA((1,))],
        flops=2 * 16 * 512 * 8192,
        size=9 << 20,
        aliases={6: 0},
    )(tile_source, tile_count, one, scaling, edge_tiles, front, agg)
    two = exchange(send)

    shifts = jnp.arange(32, dtype=jnp.int32)
    bits = jnp.bitwise_and(jnp.right_shift(drop_bits[:, :, None], shifts), 1)
    keep = (bits.reshape(drop_bits.shape[0], hidden_width).astype(F32) * 2.0).T
    core = (lax.axis_index("dp") % 2).reshape(1)
    wide = (hidden_width, width)
    pre, back = call(
        early_kernel, "early", [VMEM, VMEM, VMEM, VMEM], [(wide, F32), (wide, F32)], flops=400 << 20, size=4 << 20
    )(mine, one, self_first.T, self_second)
    gt = pltpu.VMEM((owners, cols, width), BF)
    ys, xs = replicas // 2, 4
    zs = owners // xs
    half = ((ys, owners, rows, 128), BF)
    send, hidden, d_pre = call(
        send_kernel,
        "send",
        [SMEM, HBM, VMEM, VMEM, HBM, HBM, VMEM, HBM, HBM],
        [half, (wide, BF, HBM), (wide, BF, HBM)],
        [
            gt,
            pltpu.VMEM(wide, F32),
            pltpu.VMEM(wide, F32),
            pltpu.VMEM((hidden_width, self_first.shape[0]), BF),
            pltpu.VMEM((hidden_width, hidden_width), BF),
            pltpu.VMEM(wide, BF),
            pltpu.VMEM(wide, BF),
            DMA((5,)),
            DMA((2,)),
        ],
        flops=800 << 20,
        size=6 << 20,
    )(core, mine, one, two, pre, back, keep, neigh_first.T, neigh_second)
    swap = [(i, i ^ 1) for i in range(replicas)]
    other = lax.ppermute(send, "dp", swap)
    (kept,) = call(
        keep_kernel,
        "keep",
        [SMEM, HBM, VMEM, VMEM, HBM, HBM],
        [half],
        [gt, pltpu.VMEM(wide, BF), pltpu.VMEM(wide, BF), DMA((3,))],
        flops=400 << 20,
        size=3 << 20,
    )(core, mine, one, two, hidden, d_pre)

    def trade(value, member):
        flips = (1, 3)
        pairs = []
        for y in range(ys):
            for c in range(2):
                for x in range(xs):
                    there = ((y ^ (flips[c] * (member // 2))) * 2 + c) * owners + (x ^ (flips[c] * (member % 2))) * zs
                    here = (2 * y + c) * owners + x * zs
                    pairs += [(here + z, there + z) for z in range(zs)]
        return lax.ppermute(value, ("dp", "feat"), pairs)

    def ordered(at, flip):
        return jnp.stack([jnp.minimum(at, at ^ flip), jnp.maximum(at, at ^ flip)])

    x, y = lax.axis_index("feat") // zs, lax.axis_index("dp") // 2
    near = jnp.where(core[0] == 0, 1, 3)
    slots = [
        ordered(y ^ (near * (m // 2)), near ^ 2)[:, None] * xs + ordered(x ^ (near * (m % 2)), near ^ 2)[None]
        for m in range(4)
    ]
    parts = (ys * xs, zs, rows, 128)
    four = ((4,) + parts[1:], BF)
    own, *sends = call(pair_kernel, "pair", [SMEM, VMEM, VMEM], [four] * 4, size=5 << 20)(
        jnp.stack(slots).reshape(ys * xs).astype(jnp.int32), kept.reshape(parts), other.reshape(parts)
    )
    got = [trade(sends[m - 1], m) for m in (1, 2, 3)]
    (own,) = call(square_kernel, "square", [VMEM] * 4, [four], size=2 << 20)(own, *got)
    lines = (((0, 3), (1, 2)), ((0, 1), (2, 3)))
    groups = [
        [(2 * y + c) * owners + x * zs + z for y in line for x in row for z in range(zs)]
        for c in range(2)
        for line in lines[c]
        for row in lines[c]
    ]
    shares = lax.all_to_all(
        own.reshape(4 * zs, rows, 128), ("dp", "feat"), 0, 0, tiled=True, axis_index_groups=groups
    )
    share = jnp.sum(shares.astype(F32), axis=0)
    both = jnp.stack([share, lax.ppermute(share, "dp", swap)])
    moved = {0: both}
    for k in (1, 3, 2):
        moved[k] = lax.ppermute(both, "dp", [(i, ((i // 2 + k) % ys) * 2 + i % 2) for i in range(replicas)])
    where = jnp.concatenate([core, (lax.axis_index("dp") // 2).reshape(1)])
    return tuple(
        call(
            place_kernel,
            "place",
            [SMEM] + [VMEM] * ys,
            [((r, hidden_width), F32) for r in (feats, feats, cols, cols)],
        )(where, *(moved[k] for k in range(ys)))
    )


def solution(mesh):
    return jax.shard_map(
        functools.partial(local, owners=mesh.shape["feat"], replicas=mesh.shape["dp"]),
        mesh=mesh,
        in_specs=(
            P("feat", "dp"),
            P("dp", None, None, None),
            P("dp", None),
            P("dp"),
            P(("dp", "feat"), None),
            P(("dp", "feat"), None),
            P(),
            P(),
            P(),
            P(),
        ),
        out_specs=(P("feat", None), P("feat", None), P("feat", None), P("feat", None)),
        check_vma=False,
    )
```

```python
import functools

import jax
import jax.numpy as jnp
from jax import lax
from jax.experimental import pallas as pl
from jax.experimental.pallas import tpu as pltpu
from jax.sharding import PartitionSpec as P

BF = jnp.bfloat16
F32 = jnp.float32
STEP = 8
FRONT = 16
FEATS = 32
LAST = (((1,), (1,)), ((), ()))


def alive(count, slot):
    return jnp.where(slot < count, 1.0, 0.0).astype(F32)


def begin(pairs, sems):
    copies = [pltpu.make_async_copy(src, dst, sems.at[i]) for i, (src, dst) in enumerate(pairs)]
    for copy in copies:
        copy.start()
    return copies


def chunk(tiles_ref, held_ref, sems, i):
    part = pl.ds(i * STEP, STEP)
    return pltpu.make_async_copy(tiles_ref.at[part], held_ref.at[part], sems.at[i])


def prep_kernel(x_ref, g_ref, out_ref, x_held, g_held, sems):
    owners, rows, width = out_ref.shape
    copies = begin([(g_ref, g_held), (x_ref, x_held)], sems)
    copies[0].wait()
    out_ref[:, FEATS:, :] = g_held[...].T.reshape(owners, rows - FEATS, width)
    copies[1].wait()
    for o in range(owners):
        out_ref[o, :FEATS, :] = x_held[:, o * width : (o + 1) * width]


def agg_kernel(source_ref, count_ref, x_ref, tiles_ref, agg_ref, scale_ref, front_ref, x_held, held_ref, x_sem, sems):
    blocks, slots, side, _ = held_ref.shape
    steps = blocks // STEP
    copies = begin([(x_ref, x_held)], x_sem)
    for i in range(steps):
        chunk(tiles_ref, held_ref, sems, i).start()
    copies[0].wait()

    @pl.loop(0, steps)
    def _(i):
        chunk(tiles_ref, held_ref, sems, i).wait()
        for j in range(STEP):
            b = i * STEP + j
            count = count_ref[b]
            parts = []
            for t in range(slots):
                start = pl.multiple_of(source_ref[b, t] * side, side)
                x = jnp.concatenate([x_held[:, pl.ds(start, side)], jnp.ones((16, side), BF)], axis=0)
                parts.append(x * jnp.full((FEATS + 16, side), alive(count, t), F32).astype(BF))
            lhs = jnp.concatenate(parts, axis=1)
            rhs = jnp.concatenate([held_ref[b, t] for t in range(slots)], axis=1)
            out = lax.dot_general(lhs, rhs, LAST, preferred_element_type=F32)
            scale = lax.rsqrt(out[FEATS : FEATS + 1])
            agg_ref[b // 2, :FEATS, (j % 2) * side : (j % 2 + 1) * side] = (out[:FEATS] * scale).astype(BF)
            scale_ref[pl.ds(b, 1)] = scale

    front_ref[...] = held_ref[: front_ref.shape[0]]


def back_kernel(
    source_ref, count_ref, one_ref, scale_ref, tiles_ref, front_ref, agg_ref, out_ref, acc_ref, q_ref, held_ref, sems, out_sem
):
    blocks, slots, side, _ = held_ref.shape
    steps, first = blocks // STEP, front_ref.shape[0] // STEP
    for i in range(first, steps):
        chunk(tiles_ref, held_ref, sems, i).start()
    acc_ref[...] = jnp.zeros_like(acc_ref)

    def add_up(i, tiles):
        for j in range(STEP):
            b = i * STEP + j
            count = count_ref[b]
            g = one_ref[b // 2, FEATS:, (j % 2) * side : (j % 2 + 1) * side].astype(F32)
            g = (g * scale_ref[pl.ds(b, 1)]).astype(BF)
            rhs = jnp.concatenate([tiles[b, t] for t in range(slots)], axis=1)
            out = jnp.dot(g, rhs, preferred_element_type=F32)
            for t in range(slots):
                src = source_ref[b, t]
                acc_ref[src] = acc_ref[src] + out[:, t * side : (t + 1) * side] * alive(count, t)

    @pl.loop(0, first)
    def _(i):
        add_up(i, front_ref)

    @pl.loop(first, steps)
    def _(i):
        chunk(tiles_ref, held_ref, sems, i).wait()
        add_up(i, held_ref)

    for o in range(q_ref.shape[0]):
        q_ref[o, :, :side] = acc_ref[2 * o].astype(BF)
        q_ref[o, :, side:] = acc_ref[2 * o + 1].astype(BF)
    begin([(q_ref, out_ref.at[:, FEATS:, :])], out_sem)[0].wait()


def upper(ref):
    owners, _, width = ref.shape
    return ref[:, :FEATS, :].reshape(owners * FEATS, width)


def lower(ref):
    owners, rows, width = ref.shape
    return ref[:, FEATS:, :].reshape(owners * (rows - FEATS), width)


def early_kernel(mine_ref, one_ref, wsf_ref, wss_ref, pre_ref, back_ref):
    pre_ref[...] = jnp.dot(wsf_ref[...], upper(one_ref), preferred_element_type=F32)
    back_ref[...] = jnp.dot(wss_ref[...], lower(mine_ref), preferred_element_type=F32)


def write_half(half, gt_ref, one_ref, two_ref, hidden, d_pre, out_ref, done=None):
    ys, owners, rows, lanes = out_ref.shape
    if half:
        left, right = upper(two_ref), lower(two_ref)
    else:
        left, right = upper(one_ref), gt_ref[...].reshape(hidden.shape)
    second = lax.dot_general(hidden, right, LAST, preferred_element_type=F32).astype(BF)
    for y in range(ys):
        out_ref[y, :, FEATS:, :] = second[:, y * lanes : (y + 1) * lanes].reshape(owners, rows - FEATS, lanes)
    for part in range(2):
        span = ys // 2 * lanes
        first = lax.dot_general(left, d_pre[part * span : (part + 1) * span], LAST, preferred_element_type=F32)
        first = first.astype(BF)
        for i in range(ys // 2):
            cut = first[:, i * lanes : (i + 1) * lanes]
            out_ref[part * (ys // 2) + i, :, :FEATS, :] = cut.reshape(owners, FEATS, lanes)
        if done is not None:
            done(part)


def send_kernel(
    core_ref,
    mine_ref,
    one_ref,
    two_ref,
    pre_ref,
    back_ref,
    keep_ref,
    wnf_ref,
    wns_ref,
    send_out,
    hidden_out,
    d_pre_out,
    gt_held,
    pre_held,
    back_held,
    wnf_held,
    wns_held,
    hidden_ref,
    d_pre_ref,
    send_ref,
    sems,
    out_sems,
    send_sems,
):
    copies = begin(
        [
            (wnf_ref, wnf_held),
            (pre_ref, pre_held),
            (wns_ref, wns_held),
            (back_ref, back_held),
            (mine_ref.at[:, FEATS:, :], gt_held),
        ],
        sems,
    )
    copies[0].wait()
    pre = jnp.dot(wnf_held[...], upper(two_ref), preferred_element_type=F32)
    copies[1].wait()
    pre = pre + pre_held[...]
    hidden_width, width = pre.shape
    side = width // 2
    keep = jnp.concatenate(
        [
            jnp.broadcast_to(keep_ref[:, 0:1], (hidden_width, side)),
            jnp.broadcast_to(keep_ref[:, 1:2], (hidden_width, side)),
        ],
        axis=1,
    )
    sigma = jax.nn.sigmoid(pre)
    hidden_ref[...] = (pre * sigma * keep).astype(BF)
    slope = sigma * (1.0 + pre * (1.0 - sigma)) * keep
    copies[2].wait()
    back = jnp.dot(wns_held[...], lower(two_ref), preferred_element_type=F32)
    copies[3].wait()
    d_pre_ref[...] = ((back + back_held[...]) * slope).astype(BF)
    copies[4].wait()
    leaving = begin([(hidden_ref, hidden_out), (d_pre_ref, d_pre_out)], out_sems)
    span = send_ref.shape[0] // 2
    parts = [
        pltpu.make_async_copy(send_ref.at[pl.ds(i * span, span)], send_out.at[pl.ds(i * span, span)], send_sems.at[i])
        for i in range(2)
    ]
    for core in range(2):

        @pl.when(core_ref[0] == core)
        def _():
            write_half(
                1 - core,
                gt_held,
                one_ref,
                two_ref,
                hidden_ref[...],
                d_pre_ref[...],
                send_ref,
                lambda part: parts[part].start(),
            )

    for copy in leaving + parts:
        copy.wait()


def keep_kernel(core_ref, mine_ref, one_ref, two_ref, hidden_ref, d_pre_ref, keep_ref, gt_held, hidden, d_pre, sems):
    copies = begin(
        [(d_pre_ref, d_pre), (hidden_ref, hidden), (mine_ref.at[:, FEATS:, :], gt_held)], sems
    )
    for copy in copies:
        copy.wait()
    for core in range(2):

        @pl.when(core_ref[0] == core)
        def _():
            write_half(core, gt_held, one_ref, two_ref, hidden[...], d_pre[...], keep_ref)


def add(*terms):
    total = terms[0].astype(F32)
    for term in terms[1:]:
        total = total + term.astype(F32)
    return total.astype(BF)


def pair_kernel(slot_ref, keep_ref, other_ref, *outs):
    for i, out in enumerate(outs):
        for j in range(4):
            slot = slot_ref[4 * i + j]
            out[j] = add(keep_ref[slot], other_ref[slot])


def square_kernel(own_ref, got_one, got_two, got_three, out_ref):
    out_ref[...] = add(own_ref[...], got_one[...], got_two[...], got_three[...])


def place_kernel(where_ref, *refs):
    ins, outs = refs[:4], refs[4:]
    ys = len(ins)
    for core in range(2):

        @pl.when(where_ref[0] == core)
        def _():
            for k in range(ys):
                start = pl.multiple_of(lax.rem(where_ref[1] + ys - k, ys) * 128, 128)
                for r in range(2):
                    half = core ^ r
                    outs[half][:, pl.ds(start, 128)] = ins[k][r, :FEATS]
                    outs[2 + half][:, pl.ds(start, 128)] = ins[k][r, FEATS:]


SMEM = pl.BlockSpec(memory_space=pltpu.SMEM)
VMEM = pl.BlockSpec(memory_space=pltpu.VMEM)
HBM = pl.BlockSpec(memory_space=pltpu.HBM)
DMA = pltpu.SemaphoreType.DMA


def call(kernel, name, ins, outs, scratch=(), flops=0, size=1 << 20, aliases=None):
    run = pl.pallas_call(
        kernel,
        in_specs=list(ins),
        out_specs=[o[2] if len(o) > 2 else VMEM for o in outs],
        out_shape=[
            ((pltpu.HBM if o[2] is HBM else pltpu.VMEM) if len(o) > 2 else jax.ShapeDtypeStruct)(*o[:2]) for o in outs
        ],
        scratch_shapes=list(scratch),
        input_output_aliases=aliases or {},
        compiler_params=pltpu.CompilerParams(vmem_limit_bytes=24 << 20),
        cost_estimate=pl.CostEstimate(flops=flops, bytes_accessed=size, transcendentals=0),
        name=name,
    )

    def apply(*args):
        return run(
            *(
                pltpu.with_memory_space_constraint(a, pltpu.HBM) if spec is HBM else a
                for a, spec in zip(args, ins, strict=True)
            )
        )

    return apply


def local(
    node_features,
    edge_tiles,
    tile_source,
    tile_count,
    drop_bits,
    cotangent,
    self_first,
    neigh_first,
    self_second,
    neigh_second,
    owners,
    replicas,
):
    blocks, slots, side, _ = edge_tiles.shape
    feats, nodes = node_features.shape
    width = nodes // owners
    hidden_width = self_first.shape[1]
    cols = hidden_width // owners
    rows = feats + cols
    steps = blocks // STEP
    exchange = functools.partial(lax.all_to_all, axis_name="feat", split_axis=0, concat_axis=0, tiled=True)

    (mine,) = call(
        prep_kernel,
        "prep",
        [HBM] * 2,
        [((owners, rows, width), BF)],
        [pltpu.VMEM((feats, nodes), BF), pltpu.VMEM((width, hidden_width), BF), DMA((2,))],
    )(node_features, cotangent)
    one = exchange(mine)
    held = pltpu.VMEM((blocks, slots, side, side), BF)
    agg, scaling, front = call(
        agg_kernel,
        "agg",
        [SMEM, SMEM, HBM, HBM],
        [((owners, rows, width), BF), ((blocks, side), F32), ((FRONT,) + edge_tiles.shape[1:], BF, VMEM)],
        [pltpu.VMEM((feats, nodes), BF), held, DMA((1,)), DMA((steps,))],
        flops=2 * 48 * 512 * 8192,
        size=9 << 20,
    )(tile_source, tile_count, node_features, edge_tiles)
    (send,) = call(
        back_kernel,
        "back",
        [SMEM, SMEM, VMEM, VMEM, HBM, VMEM, HBM],
        [((owners, rows, width), BF, HBM)],
        [pltpu.VMEM((blocks, cols, side), F32), pltpu.VMEM((owners, cols, width), BF), held, DMA((steps,)), DMA((1,))],
        flops=2 * 16 * 512 * 8192,
        size=9 << 20,
        aliases={6: 0},
    )(tile_source, tile_count, one, scaling, edge_tiles, front, agg)
    two = exchange(send)

    shifts = jnp.arange(32, dtype=jnp.int32)
    bits = jnp.bitwise_and(jnp.right_shift(drop_bits[:, :, None], shifts), 1)
    keep = (bits.reshape(drop_bits.shape[0], hidden_width).astype(F32) * 2.0).T
    core = (lax.axis_index("dp") % 2).reshape(1)
    wide = (hidden_width, width)
    pre, back = call(
        early_kernel, "early", [VMEM, VMEM, VMEM, VMEM], [(wide, F32), (wide, F32)], flops=400 << 20, size=4 << 20
    )(mine, one, self_first.T, self_second)
    gt = pltpu.VMEM((owners, cols, width), BF)
    ys, xs = replicas // 2, 4
    zs = owners // xs
    half = ((ys, owners, rows, 128), BF)
    send, hidden, d_pre = call(
        send_kernel,
        "send",
        [SMEM, HBM, VMEM, VMEM, HBM, HBM, VMEM, HBM, HBM],
        [half + (HBM,), (wide, BF, HBM), (wide, BF, HBM)],
        [
            gt,
            pltpu.VMEM(wide, F32),
            pltpu.VMEM(wide, F32),
            pltpu.VMEM((hidden_width, self_first.shape[0]), BF),
            pltpu.VMEM((hidden_width, hidden_width), BF),
            pltpu.VMEM(wide, BF),
            pltpu.VMEM(wide, BF),
            pltpu.VMEM(*half),
            DMA((5,)),
            DMA((2,)),
            DMA((2,)),
        ],
        flops=800 << 20,
        size=6 << 20,
    )(core, mine, one, two, pre, back, keep, neigh_first.T, neigh_second)
    swap = [(i, i ^ 1) for i in range(replicas)]
    other = lax.ppermute(send, "dp", swap)
    (kept,) = call(
        keep_kernel,
        "keep",
        [SMEM, HBM, VMEM, VMEM, HBM, HBM],
        [half],
        [gt, pltpu.VMEM(wide, BF), pltpu.VMEM(wide, BF), DMA((3,))],
        flops=400 << 20,
        size=3 << 20,
    )(core, mine, one, two, hidden, d_pre)

    def trade(value, member):
        flips = (1, 3)
        pairs = []
        for y in range(ys):
            for c in range(2):
                for x in range(xs):
                    there = ((y ^ (flips[c] * (member // 2))) * 2 + c) * owners + (x ^ (flips[c] * (member % 2))) * zs
                    here = (2 * y + c) * owners + x * zs
                    pairs += [(here + z, there + z) for z in range(zs)]
        return lax.ppermute(value, ("dp", "feat"), pairs)

    def ordered(at, flip):
        return jnp.stack([jnp.minimum(at, at ^ flip), jnp.maximum(at, at ^ flip)])

    x, y = lax.axis_index("feat") // zs, lax.axis_index("dp") // 2
    near = jnp.where(core[0] == 0, 1, 3)
    slots = [
        ordered(y ^ (near * (m // 2)), near ^ 2)[:, None] * xs + ordered(x ^ (near * (m % 2)), near ^ 2)[None]
        for m in range(4)
    ]
    parts = (ys * xs, zs, rows, 128)
    four = ((4,) + parts[1:], BF)
    own, *sends = call(pair_kernel, "pair", [SMEM, VMEM, VMEM], [four] * 4, size=5 << 20)(
        jnp.stack(slots).reshape(ys * xs).astype(jnp.int32), kept.reshape(parts), other.reshape(parts)
    )
    got = [trade(sends[m - 1], m) for m in (1, 2, 3)]
    (own,) = call(square_kernel, "square", [VMEM] * 4, [four], size=2 << 20)(own, *got)
    lines = (((0, 3), (1, 2)), ((0, 1), (2, 3)))
    groups = [
        [(2 * y + c) * owners + x * zs + z for y in line for x in row for z in range(zs)]
        for c in range(2)
        for line in lines[c]
        for row in lines[c]
    ]
    shares = lax.all_to_all(
        own.reshape(4 * zs, rows, 128), ("dp", "feat"), 0, 0, tiled=True, axis_index_groups=groups
    )
    share = jnp.sum(shares.astype(F32), axis=0)
    both = jnp.stack([share, lax.ppermute(share, "dp", swap)])
    moved = {0: both}
    for k in (1, 3, 2):
        moved[k] = lax.ppermute(both, "dp", [(i, ((i // 2 + k) % ys) * 2 + i % 2) for i in range(replicas)])
    where = jnp.concatenate([core, (lax.axis_index("dp") // 2).reshape(1)])
    return tuple(
        call(
            place_kernel,
            "place",
            [SMEM] + [VMEM] * ys,
            [((r, hidden_width), F32) for r in (feats, feats, cols, cols)],
        )(where, *(moved[k] for k in range(ys)))
    )


def solution(mesh):
    return jax.shard_map(
        functools.partial(local, owners=mesh.shape["feat"], replicas=mesh.shape["dp"]),
        mesh=mesh,
        in_specs=(
            P("feat", "dp"),
            P("dp", None, None, None),
            P("dp", None),
            P("dp"),
            P(("dp", "feat"), None),
            P(("dp", "feat"), None),
            P(),
            P(),
            P(),
            P(),
        ),
        out_specs=(P("feat", None), P("feat", None), P("feat", None), P("feat", None)),
        check_vma=False,
    )
```

```python
import functools

import jax
import jax.numpy as jnp
from jax import lax
from jax.experimental import pallas as pl
from jax.experimental.pallas import tpu as pltpu
from jax.sharding import PartitionSpec as P

BF = jnp.bfloat16
F32 = jnp.float32
STEP = 8
FRONT = 16
FEATS = 32
LAST = (((1,), (1,)), ((), ()))


def alive(count, slot):
    return jnp.where(slot < count, 1.0, 0.0).astype(F32)


def begin(pairs, sems):
    copies = [pltpu.make_async_copy(src, dst, sems.at[i]) for i, (src, dst) in enumerate(pairs)]
    for copy in copies:
        copy.start()
    return copies


def chunk(tiles_ref, held_ref, sems, i):
    part = pl.ds(i * STEP, STEP)
    return pltpu.make_async_copy(tiles_ref.at[part], held_ref.at[part], sems.at[i])


def prep_kernel(x_ref, g_ref, out_ref, x_held, g_held, sems):
    owners, rows, width = out_ref.shape
    copies = begin([(g_ref, g_held), (x_ref, x_held)], sems)
    copies[0].wait()
    out_ref[:, FEATS:, :] = g_held[...].T.reshape(owners, rows - FEATS, width)
    copies[1].wait()
    for o in range(owners):
        out_ref[o, :FEATS, :] = x_held[:, o * width : (o + 1) * width]


def agg_kernel(source_ref, count_ref, x_ref, tiles_ref, agg_ref, scale_ref, front_ref, x_held, held_ref, x_sem, sems):
    blocks, slots, side, _ = held_ref.shape
    steps = blocks // STEP
    copies = begin([(x_ref, x_held)], x_sem)
    for i in range(steps):
        chunk(tiles_ref, held_ref, sems, i).start()
    copies[0].wait()

    @pl.loop(0, steps)
    def _(i):
        chunk(tiles_ref, held_ref, sems, i).wait()
        for j in range(STEP):
            b = i * STEP + j
            count = count_ref[b]
            parts = []
            for t in range(slots):
                start = pl.multiple_of(source_ref[b, t] * side, side)
                x = jnp.concatenate([x_held[:, pl.ds(start, side)], jnp.ones((16, side), BF)], axis=0)
                parts.append(x * jnp.full((FEATS + 16, side), alive(count, t), F32).astype(BF))
            lhs = jnp.concatenate(parts, axis=1)
            rhs = jnp.concatenate([held_ref[b, t] for t in range(slots)], axis=1)
            out = lax.dot_general(lhs, rhs, LAST, preferred_element_type=F32)
            scale = lax.rsqrt(out[FEATS : FEATS + 1])
            agg_ref[b // 2, :FEATS, (j % 2) * side : (j % 2 + 1) * side] = (out[:FEATS] * scale).astype(BF)
            scale_ref[pl.ds(b, 1)] = scale

    front_ref[...] = held_ref[: front_ref.shape[0]]


def back_kernel(
    source_ref, count_ref, one_ref, scale_ref, tiles_ref, front_ref, agg_ref, out_ref, acc_ref, q_ref, held_ref, sems, out_sem
):
    blocks, slots, side, _ = held_ref.shape
    steps, first = blocks // STEP, front_ref.shape[0] // STEP
    for i in range(first, steps):
        chunk(tiles_ref, held_ref, sems, i).start()
    acc_ref[...] = jnp.zeros_like(acc_ref)

    def add_up(i, tiles):
        for j in range(STEP):
            b = i * STEP + j
            count = count_ref[b]
            g = one_ref[b // 2, FEATS:, (j % 2) * side : (j % 2 + 1) * side].astype(F32)
            g = (g * scale_ref[pl.ds(b, 1)]).astype(BF)
            rhs = jnp.concatenate([tiles[b, t] for t in range(slots)], axis=1)
            out = jnp.dot(g, rhs, preferred_element_type=F32)
            for t in range(slots):
                src = source_ref[b, t]
                acc_ref[src] = acc_ref[src] + out[:, t * side : (t + 1) * side] * alive(count, t)

    @pl.loop(0, first)
    def _(i):
        add_up(i, front_ref)

    @pl.loop(first, steps)
    def _(i):
        chunk(tiles_ref, held_ref, sems, i).wait()
        add_up(i, held_ref)

    for o in range(q_ref.shape[0]):
        q_ref[o, :, :side] = acc_ref[2 * o].astype(BF)
        q_ref[o, :, side:] = acc_ref[2 * o + 1].astype(BF)
    begin([(q_ref, out_ref.at[:, FEATS:, :])], out_sem)[0].wait()


def upper(ref):
    owners, _, width = ref.shape
    return ref[:, :FEATS, :].reshape(owners * FEATS, width)


def lower(ref):
    owners, rows, width = ref.shape
    return ref[:, FEATS:, :].reshape(owners * (rows - FEATS), width)


def early_kernel(mine_ref, one_ref, wsf_ref, wss_ref, pre_ref, back_ref):
    pre_ref[...] = jnp.dot(wsf_ref[...], upper(one_ref), preferred_element_type=F32)
    back_ref[...] = jnp.dot(wss_ref[...], lower(mine_ref), preferred_element_type=F32)


def write_half(half, gt_ref, one_ref, two_ref, hidden, d_pre, out_ref):
    ys, owners, rows, lanes = out_ref.shape
    if half:
        left, right = upper(two_ref), lower(two_ref)
    else:
        left, right = upper(one_ref), gt_ref[...].reshape(hidden.shape)
    first = lax.dot_general(left, d_pre, LAST, preferred_element_type=F32).astype(BF)
    second = lax.dot_general(hidden, right, LAST, preferred_element_type=F32).astype(BF)
    for y in range(ys):
        cut = slice(y * lanes, (y + 1) * lanes)
        out_ref[y, :, :FEATS, :] = first[:, cut].reshape(owners, FEATS, lanes)
        out_ref[y, :, FEATS:, :] = second[:, cut].reshape(owners, rows - FEATS, lanes)


def send_kernel(
    core_ref,
    mine_ref,
    one_ref,
    two_ref,
    pre_ref,
    back_ref,
    keep_ref,
    wnf_ref,
    wns_ref,
    send_ref,
    hidden_out,
    d_pre_out,
    gt_held,
    pre_held,
    back_held,
    wnf_held,
    wns_held,
    hidden_ref,
    d_pre_ref,
    sems,
    out_sems,
):
    copies = begin(
        [
            (wnf_ref, wnf_held),
            (pre_ref, pre_held),
            (wns_ref, wns_held),
            (back_ref, back_held),
            (mine_ref.at[:, FEATS:, :], gt_held),
        ],
        sems,
    )
    copies[0].wait()
    pre = jnp.dot(wnf_held[...], upper(two_ref), preferred_element_type=F32)
    copies[1].wait()
    pre = pre + pre_held[...]
    hidden_width, width = pre.shape
    side = width // 2
    keep = jnp.concatenate(
        [
            jnp.broadcast_to(keep_ref[:, 0:1], (hidden_width, side)),
            jnp.broadcast_to(keep_ref[:, 1:2], (hidden_width, side)),
        ],
        axis=1,
    )
    sigma = jax.nn.sigmoid(pre)
    hidden_ref[...] = (pre * sigma * keep).astype(BF)
    slope = sigma * (1.0 + pre * (1.0 - sigma)) * keep
    copies[2].wait()
    back = jnp.dot(wns_held[...], lower(two_ref), preferred_element_type=F32)
    copies[3].wait()
    d_pre_ref[...] = ((back + back_held[...]) * slope).astype(BF)
    copies[4].wait()
    leaving = begin([(hidden_ref, hidden_out), (d_pre_ref, d_pre_out)], out_sems)
    for core in range(2):

        @pl.when(core_ref[0] == core)
        def _():
            write_half(1 - core, gt_held, one_ref, two_ref, hidden_ref[...], d_pre_ref[...], send_ref)

    for copy in leaving:
        copy.wait()


def keep_kernel(core_ref, mine_ref, one_ref, two_ref, hidden_ref, d_pre_ref, keep_ref, gt_held, hidden, d_pre, sems):
    copies = begin(
        [(d_pre_ref, d_pre), (hidden_ref, hidden), (mine_ref.at[:, FEATS:, :], gt_held)], sems
    )
    for copy in copies:
        copy.wait()
    for core in range(2):

        @pl.when(core_ref[0] == core)
        def _():
            write_half(core, gt_held, one_ref, two_ref, hidden[...], d_pre[...], keep_ref)


def add(*terms):
    total = terms[0].astype(F32)
    for term in terms[1:]:
        total = total + term.astype(F32)
    return total.astype(BF)


def pair_kernel(slot_ref, keep_ref, other_ref, *outs):
    for i, out in enumerate(outs):
        for j in range(4):
            slot = slot_ref[4 * i + j]
            out[j] = add(keep_ref[slot], other_ref[slot])


def square_kernel(own_ref, got_one, got_two, got_three, out_ref):
    out_ref[...] = add(own_ref[...], got_one[...], got_two[...], got_three[...])


def place_kernel(where_ref, *refs):
    ins, outs = refs[:4], refs[4:]
    ys = len(ins)
    for core in range(2):

        @pl.when(where_ref[0] == core)
        def _():
            for k in range(ys):
                start = pl.multiple_of(lax.rem(where_ref[1] + ys - k, ys) * 128, 128)
                for r in range(2):
                    half = core ^ r
                    outs[half][:, pl.ds(start, 128)] = ins[k][r, :FEATS]
                    outs[2 + half][:, pl.ds(start, 128)] = ins[k][r, FEATS:]


SMEM = pl.BlockSpec(memory_space=pltpu.SMEM)
VMEM = pl.BlockSpec(memory_space=pltpu.VMEM)
HBM = pl.BlockSpec(memory_space=pltpu.HBM)
DMA = pltpu.SemaphoreType.DMA


def call(kernel, name, ins, outs, scratch=(), flops=0, size=1 << 20, aliases=None):
    run = pl.pallas_call(
        kernel,
        in_specs=list(ins),
        out_specs=[o[2] if len(o) > 2 else VMEM for o in outs],
        out_shape=[
            ((pltpu.HBM if o[2] is HBM else pltpu.VMEM) if len(o) > 2 else jax.ShapeDtypeStruct)(*o[:2]) for o in outs
        ],
        scratch_shapes=list(scratch),
        input_output_aliases=aliases or {},
        compiler_params=pltpu.CompilerParams(vmem_limit_bytes=24 << 20),
        cost_estimate=pl.CostEstimate(flops=flops, bytes_accessed=size, transcendentals=0),
        name=name,
    )

    def apply(*args):
        return run(
            *(
                pltpu.with_memory_space_constraint(a, pltpu.HBM) if spec is HBM else a
                for a, spec in zip(args, ins, strict=True)
            )
        )

    return apply


def local(
    node_features,
    edge_tiles,
    tile_source,
    tile_count,
    drop_bits,
    cotangent,
    self_first,
    neigh_first,
    self_second,
    neigh_second,
    owners,
    replicas,
):
    blocks, slots, side, _ = edge_tiles.shape
    feats, nodes = node_features.shape
    width = nodes // owners
    hidden_width = self_first.shape[1]
    cols = hidden_width // owners
    rows = feats + cols
    steps = blocks // STEP
    exchange = functools.partial(lax.all_to_all, axis_name="feat", split_axis=0, concat_axis=0, tiled=True)

    (mine,) = call(
        prep_kernel,
        "prep",
        [HBM] * 2,
        [((owners, rows, width), BF)],
        [pltpu.VMEM((feats, nodes), BF), pltpu.VMEM((width, hidden_width), BF), DMA((2,))],
    )(node_features, cotangent)
    one = exchange(mine)
    held = pltpu.VMEM((blocks, slots, side, side), BF)
    agg, scaling, front = call(
        agg_kernel,
        "agg",
        [SMEM, SMEM, HBM, HBM],
        [((owners, rows, width), BF), ((blocks, side), F32), ((FRONT,) + edge_tiles.shape[1:], BF, VMEM)],
        [pltpu.VMEM((feats, nodes), BF), held, DMA((1,)), DMA((steps,))],
        flops=2 * 48 * 512 * 8192,
        size=9 << 20,
    )(tile_source, tile_count, node_features, edge_tiles)
    (send,) = call(
        back_kernel,
        "back",
        [SMEM, SMEM, VMEM, VMEM, HBM, VMEM, HBM],
        [((owners, rows, width), BF, HBM)],
        [pltpu.VMEM((blocks, cols, side), F32), pltpu.VMEM((owners, cols, width), BF), held, DMA((steps,)), DMA((1,))],
        flops=2 * 16 * 512 * 8192,
        size=9 << 20,
        aliases={6: 0},
    )(tile_source, tile_count, one, scaling, edge_tiles, front, agg)
    two = exchange(send)

    shifts = jnp.arange(32, dtype=jnp.int32)
    bits = jnp.bitwise_and(jnp.right_shift(drop_bits[:, :, None], shifts), 1)
    keep = (bits.reshape(drop_bits.shape[0], hidden_width).astype(F32) * 2.0).T
    core = (lax.axis_index("dp") % 2).reshape(1)
    wide = (hidden_width, width)
    pre, back = call(
        early_kernel, "early", [VMEM, VMEM, VMEM, VMEM], [(wide, F32), (wide, F32)], flops=400 << 20, size=4 << 20
    )(mine, one, self_first.T, self_second)
    gt = pltpu.VMEM((owners, cols, width), BF)
    ys, xs = replicas // 2, 4
    zs = owners // xs
    half = ((ys, owners, rows, 128), BF)
    send, hidden, d_pre = call(
        send_kernel,
        "send",
        [SMEM, HBM, VMEM, VMEM, HBM, HBM, VMEM, HBM, HBM],
        [half, (wide, BF, HBM), (wide, BF, HBM)],
        [
            gt,
            pltpu.VMEM(wide, F32),
            pltpu.VMEM(wide, F32),
            pltpu.VMEM((hidden_width, self_first.shape[0]), BF),
            pltpu.VMEM((hidden_width, hidden_width), BF),
            pltpu.VMEM(wide, BF),
            pltpu.VMEM(wide, BF),
            DMA((5,)),
            DMA((2,)),
        ],
        flops=800 << 20,
        size=6 << 20,
    )(core, mine, one, two, pre, back, keep, neigh_first.T, neigh_second)
    swap = [(i, i ^ 1) for i in range(replicas)]
    other = lax.ppermute(send, "dp", swap)
    (kept,) = call(
        keep_kernel,
        "keep",
        [SMEM, HBM, VMEM, VMEM, HBM, HBM],
        [half],
        [gt, pltpu.VMEM(wide, BF), pltpu.VMEM(wide, BF), DMA((3,))],
        flops=400 << 20,
        size=3 << 20,
    )(core, mine, one, two, hidden, d_pre)

    def trade(value, member):
        flips = (1, 3)
        pairs = []
        for y in range(ys):
            for c in range(2):
                for x in range(xs):
                    there = ((y ^ (flips[c] * (member // 2))) * 2 + c) * owners + (x ^ (flips[c] * (member % 2))) * zs
                    here = (2 * y + c) * owners + x * zs
                    pairs += [(here + z, there + z) for z in range(zs)]
        return lax.ppermute(value, ("dp", "feat"), pairs)

    def ordered(at, flip):
        return jnp.stack([jnp.minimum(at, at ^ flip), jnp.maximum(at, at ^ flip)])

    x, y = lax.axis_index("feat") // zs, lax.axis_index("dp") // 2
    near = jnp.where(core[0] == 0, 1, 3)
    slots = [
        ordered(y ^ (near * (m // 2)), near ^ 2)[:, None] * xs + ordered(x ^ (near * (m % 2)), near ^ 2)[None]
        for m in range(4)
    ]
    parts = (ys * xs, zs, rows, 128)
    four = ((4,) + parts[1:], BF)
    own, *sends = call(pair_kernel, "pair", [SMEM, VMEM, VMEM], [four] * 4, size=5 << 20)(
        jnp.stack(slots).reshape(ys * xs).astype(jnp.int32), kept.reshape(parts), other.reshape(parts)
    )
    got = [trade(sends[m - 1], m) for m in (3, 1, 2)]
    (own,) = call(square_kernel, "square", [VMEM] * 4, [four], size=2 << 20)(own, *got)
    lines = (((0, 3), (1, 2)), ((0, 1), (2, 3)))
    groups = [
        [(2 * y + c) * owners + x * zs + z for y in line for x in row for z in range(zs)]
        for c in range(2)
        for line in lines[c]
        for row in lines[c]
    ]
    shares = lax.all_to_all(
        own.reshape(4 * zs, rows, 128), ("dp", "feat"), 0, 0, tiled=True, axis_index_groups=groups
    )
    share = jnp.sum(shares.astype(F32), axis=0)
    both = jnp.stack([share, lax.ppermute(share, "dp", swap)])
    moved = {0: both}
    for k in (1, 3, 2):
        moved[k] = lax.ppermute(both, "dp", [(i, ((i // 2 + k) % ys) * 2 + i % 2) for i in range(replicas)])
    where = jnp.concatenate([core, (lax.axis_index("dp") // 2).reshape(1)])
    return tuple(
        call(
            place_kernel,
            "place",
            [SMEM] + [VMEM] * ys,
            [((r, hidden_width), F32) for r in (feats, feats, cols, cols)],
        )(where, *(moved[k] for k in range(ys)))
    )


def solution(mesh):
    return jax.shard_map(
        functools.partial(local, owners=mesh.shape["feat"], replicas=mesh.shape["dp"]),
        mesh=mesh,
        in_specs=(
            P("feat", "dp"),
            P("dp", None, None, None),
            P("dp", None),
            P("dp"),
            P(("dp", "feat"), None),
            P(("dp", "feat"), None),
            P(),
            P(),
            P(),
            P(),
        ),
        out_specs=(P("feat", None), P("feat", None), P("feat", None), P("feat", None)),
        check_vma=False,
    )
```
